256 devices in a mesh: member: 8 (over y, core), grid: 32 (over x, z).
Axes of the slice: x: 4, y: 4, z: 8, core: 2. Of those that a mesh axis runs over, the one named last changes fastest.
Arguments:
- predictions: float32 [8, 100, 32768], P('member', None, 'grid'), may hold values from -6 to 6
- truth: float32 [100, 32768], P(None, 'grid'), may hold values from -6 to 6
- area: float32 [32768], P('grid'), may hold values from 0.2 to 7.5
- queries: bfloat16 [4096, 1024], P('grid'), may hold values from -6 to 6
- cotangent: bfloat16 [8, 4096, 1024], P('member', 'grid'), may hold values from -6 to 6
- edge_slot: int32 [4096, 32], P('grid'), may hold values from 0 to 255, as said below
- edge_count: int32 [4096], P('grid'), may hold values from 2 to 32, as said below
- edge_bias: float32 [4096, 512], P('grid'), may hold values from -6 to 326
- send_rows: int32 [32, 32, 8], P('grid'), may hold values from 0 to 1023, as said below
- w_embed: bfloat16 [100, 1024], replicated, may hold values from -0.625 to 0.625
- w_query: bfloat16 [1024, 1024], replicated, may hold values from -0.1875 to 0.1875
- w_keyval: bfloat16 [1024, 2048], replicated, may hold values from -0.1875 to 0.1875
- w_out: bfloat16 [1024, 1024], replicated, may hold values from -0.1875 to 0.1875
Outputs:
- hidden: bfloat16 [8, 4096, 1024], P('member', 'grid')
- grad_pred: float32 [8, 100, 32768], P('member', None, 'grid')
- loss: float32 [], replicated
The draws below stay inside these ranges and needn't reach their ends.
Inputs may be any that keep to these rules, and one draw needn't show every extreme that they name: `send_rows`: each sending tile names 8 rows for each owner; all rows a tile sends are distinct. `edge_slot`: slots of the owner's received rows; the slots of one node are distinct. `edge_count`: edges at or beyond a node's count are padding.
All inputs are finite; a program needn't handle non-finite values.
Results may differ from the reference program's by a relative error of at most 0.0089.
Values may be sent and summed in bfloat16 or wider, within the bound.
A program may use at most 64 MiB of HBM per device.

```python
import math
import jax
import jax.numpy as jnp
from jax import lax

D = 1024
HEADS = 16
V = 100
P_DEV = 1024
H_DEV = 128
K = 32
C = 8
MEMBERS = 8
NPTS = 32768
NODES = 4096
SLOTS = 256
N_GRID = 32


def draw_area(key, part):
    key = jax.random.fold_in(key, 7)
    tile_count = NPTS // P_DEV
    tile = (jnp.arange(NPTS) // P_DEV).astype(jnp.float32)
    rising = 1.0 + 2.0 * tile / max(tile_count - 1, 1)
    rough = jax.random.uniform(key, (NPTS,), jnp.float32, 0.5, 1.5)
    return rising * rough


def draw_edge_bias(key, part):
    key = jax.random.fold_in(key, 11)
    first_key = jax.random.fold_in(key, 0)
    base = jnp.clip(jax.random.normal(first_key, (NODES, K * HEADS), jnp.float32), -6.0, 6.0)
    return base


def draw_send_rows(key, part):
    key = jax.random.fold_in(key, 5)
    source_keys = jax.random.split(key, N_GRID)

    def one_source(source_key):
        order = jax.random.permutation(source_key, P_DEV).astype(jnp.int32)
        order = jnp.where(order == P_DEV - 1, order[0], order).at[0].set(P_DEV - 1)
        order = jnp.where(order == 0, order[1], order).at[1].set(0)
        return order[:N_GRID * C].reshape(N_GRID, C)
    return jax.vmap(one_source)(source_keys)


def draw_edge_slot(key, part):
    key = jax.random.fold_in(key, 9)
    node_keys = jax.random.split(key, NODES)

    def one_node(node_key):
        order = jax.random.permutation(node_key, SLOTS).astype(jnp.int32)
        forced = jnp.where(order == SLOTS - 1, order[0], order).at[0].set(SLOTS - 1)
        forced = jnp.where(forced == 0, forced[1], forced).at[1].set(0)
        return (order[:K], forced[:K])
    drawn, forced = jax.vmap(one_node)(node_keys)
    marked = (jnp.arange(NODES) % H_DEV == 0)[:, None]
    return jnp.where(marked, forced, drawn).astype(jnp.int32)


def draw_edge_count(key, part):
    key = jax.random.fold_in(key, 13)
    counts = jax.random.randint(key, (NODES,), 2, K + 1).astype(jnp.int32)
    nodes = jnp.arange(NODES) % H_DEV
    counts = jnp.where(nodes == 0, K, jnp.where(nodes == 1, 2, counts))
    return counts.astype(jnp.int32)


def block_scale(rng, extent, cuts, low, high):
    factor_of, own = 1.0, jax.random.fold_in(rng, 6)
    for dim, blocks in cuts:
        steps = jnp.exp(jax.random.uniform(jax.random.fold_in(own, dim), (blocks,), jnp.float32, low / len(cuts), high / len(cuts)))
        factor_of = factor_of * jnp.repeat(steps, extent[dim] // blocks).reshape([-1 if axis == dim else 1 for axis in range(len(extent))])
    return factor_of


def gaussian(own_key, extent, scale, limit, cuts=(), kind=jnp.bfloat16):
    array = jax.random.normal(own_key, extent, jnp.float32) * scale
    if len(cuts) > 0:
        array = block_scale(own_key, extent, cuts, -0.22, 0.18) * array
    return jnp.clip(array, min=-limit, max=limit).astype(kind)


def setup_inputs(seed: int = 0) -> dict:
    streams_of = jax.random.split(jax.random.key(seed), 14)
    return {
        "predictions": gaussian(streams_of[0], (MEMBERS, V, NPTS), 1.0, 6.0, ((0, 8), (2, 32)), jnp.float32),
        "truth": gaussian(streams_of[1], (V, NPTS), 1.0, 6.0, ((1, 32),), jnp.float32),
        "area": draw_area(jax.random.fold_in(streams_of[13], 71), 0),
        "queries": gaussian(streams_of[3], (NODES, D), 1.0, 6.0, ((0, 32),)),
        "cotangent": gaussian(streams_of[4], (MEMBERS, NODES, D), 1.0, 6.0, ((0, 8), (1, 32))),
        "edge_slot": draw_edge_slot(jax.random.fold_in(streams_of[13], 71), 0),
        "edge_count": draw_edge_count(jax.random.fold_in(streams_of[13], 71), 0),
        "edge_bias": draw_edge_bias(jax.random.fold_in(streams_of[13], 71), 0),
        "send_rows": draw_send_rows(jax.random.fold_in(streams_of[13], 71), 0),
        "w_embed": gaussian(streams_of[9], (V, D), V ** -0.5, 0.625),
        "w_query": gaussian(streams_of[10], (D, D), D ** -0.5, 0.1875),
        "w_keyval": gaussian(streams_of[11], (D, 2 * D), D ** -0.5, 0.1875),
        "w_out": gaussian(streams_of[12], (D, D), D ** -0.5, 0.1875),
    }


alpha_fair = 0.95
big_negative = -1e+30

def attend_owner(queries, key_val, edge_slot, edge_count, edge_bias, cotangent, w_query, w_keyval, w_out):
    node_count, model_width = queries.shape
    edge_fan = edge_slot.shape[1]
    head_count = edge_bias.shape[1] // edge_fan
    head_size = model_width // head_count
    slot_count = key_val.shape[0]
    score_scale = 1.0 / math.sqrt(head_size)
    query_heads = jnp.dot(queries, w_query, preferred_element_type=jnp.float32).astype(jnp.bfloat16)
    query_heads = query_heads.reshape(node_count, head_count, head_size)
    key_heads = key_val[:, :model_width].reshape(slot_count, head_count, head_size)
    value_heads = key_val[:, model_width:].reshape(slot_count, head_count, head_size)
    active = jnp.arange(edge_fan)[None, :] < edge_count[:, None]
    chosen = jnp.logical_and(edge_slot[:, :, None] == jnp.arange(slot_count)[None, None, :], active[:, :, None]).astype(jnp.float32)
    bias_full = jnp.einsum('hks,hkn->hns', chosen, edge_bias.reshape(node_count, edge_fan, head_count), precision=lax.Precision.HIGHEST)
    present = (lax.optimization_barrier(jnp.sum(chosen, axis=1)) > 0.5)[:, None, :]
    scores = jnp.einsum('hnd,snd->hns', query_heads.astype(jnp.float32), key_heads.astype(jnp.float32)) * score_scale + bias_full
    scores = jnp.where(present, scores, big_negative)
    row_top = lax.optimization_barrier(jnp.max(scores, axis=-1, keepdims=True))
    exponent = jnp.where(present, jnp.exp(scores - row_top), 0.0)
    weights = exponent / lax.optimization_barrier(jnp.sum(exponent, axis=-1, keepdims=True))
    weights_low = weights.astype(jnp.bfloat16)
    attended = jnp.einsum('hns,snd->hnd', weights_low.astype(jnp.float32), value_heads.astype(jnp.float32))
    attended = attended.astype(jnp.bfloat16).reshape(node_count, model_width)
    hidden = (queries.astype(jnp.float32) + jnp.dot(attended, w_out, preferred_element_type=jnp.float32)).astype(jnp.bfloat16)
    grad_attended = lax.dot_general(cotangent, w_out, (((1,), (1,)), ((), ())), preferred_element_type=jnp.float32)
    grad_attended = grad_attended.astype(jnp.bfloat16).reshape(node_count, head_count, head_size)
    grad_weights = jnp.einsum('hnd,snd->hns', grad_attended.astype(jnp.float32), value_heads.astype(jnp.float32))
    inner = lax.optimization_barrier(jnp.sum(weights * grad_weights, axis=-1, keepdims=True))
    grad_score = (weights * (grad_weights - inner) * score_scale).astype(jnp.bfloat16)
    grad_keys = jnp.einsum('hns,hnd->snd', grad_score.astype(jnp.float32), query_heads.astype(jnp.float32)).astype(jnp.bfloat16)
    grad_values = jnp.einsum('hns,hnd->snd', weights_low.astype(jnp.float32), grad_attended.astype(jnp.float32)).astype(jnp.bfloat16)
    grad_kv = jnp.concatenate([grad_keys.reshape(slot_count, model_width), grad_values.reshape(slot_count, model_width)], axis=1)
    slot_grad = lax.dot_general(grad_kv, w_keyval, (((1,), (1,)), ((), ())), preferred_element_type=jnp.float32).astype(jnp.bfloat16)
    return (hidden, slot_grad)

def reference(predictions, truth, area, queries, cotangent, edge_slot, edge_count, edge_bias, send_rows, w_embed, w_query, w_keyval, w_out):
    member_count = predictions.shape[0]
    index_table = (jnp.arange(N_GRID, dtype=jnp.int32)[:, None, None] * P_DEV + send_rows).astype(jnp.int32)
    index_table = jnp.transpose(index_table, (1, 0, 2)).reshape(N_GRID, N_GRID * C)
    owner_queries = queries.reshape(N_GRID, H_DEV, D)
    owner_slots = edge_slot.reshape(N_GRID, H_DEV, K)
    owner_counts = edge_count.reshape(N_GRID, H_DEV)
    owner_bias = edge_bias.reshape(N_GRID, H_DEV, K * HEADS)
    hidden_all = []
    encoder_all = []
    for member in range(member_count):
        embedded = lax.dot_general(predictions[member].astype(jnp.bfloat16), w_embed, (((0,), (0,)), ((), ())), preferred_element_type=jnp.float32).astype(jnp.bfloat16)
        key_val = jnp.dot(embedded, w_keyval, preferred_element_type=jnp.float32).astype(jnp.bfloat16)
        owner_cot = cotangent[member].reshape(N_GRID, H_DEV, D)

        def one_owner(items):
            rows, node_q, node_slot, node_count, node_bias, node_cot = items
            return attend_owner(node_q, key_val[rows], node_slot, node_count, node_bias, node_cot, w_query, w_keyval, w_out)
        hidden_tiles, slot_grads = lax.map(one_owner, (index_table, owner_queries, owner_slots, owner_counts, owner_bias, owner_cot))
        grad_embedded = jnp.zeros((NPTS, D), jnp.float32).at[index_table.reshape(-1)].add(slot_grads.reshape(-1, D).astype(jnp.float32))
        grad_embedded = grad_embedded.astype(jnp.bfloat16)
        encoder_grad = lax.dot_general(w_embed, grad_embedded, (((1,), (1,)), ((), ())), preferred_element_type=jnp.float32)
        hidden_all.append(hidden_tiles.reshape(NODES, D))
        encoder_all.append(encoder_grad)
    coefficient = alpha_fair / (2.0 * member_count * (member_count - 1)) + (1.0 - alpha_fair) / (2.0 * member_count * member_count)
    skill = lax.optimization_barrier(jnp.mean(jnp.abs(predictions - truth[None]), axis=0))
    spread = lax.optimization_barrier(jnp.sum(jnp.abs(predictions[:, None] - predictions[None, :]), axis=(0, 1)))
    crps = skill - coefficient * spread
    total_area = jnp.sum(area)
    loss = jnp.sum(area[None, :] * crps) / (total_area * V)
    slope = jnp.sign(predictions - truth[None]) / member_count - 2.0 * coefficient * lax.optimization_barrier(jnp.sum(jnp.sign(predictions[:, None] - predictions[None, :]), axis=1))
    grad_pred = (area * NPTS / total_area)[None, None, :] * slope + jnp.stack(encoder_all)
    return (jnp.stack(hidden_all), grad_pred, loss)
```

```python
import functools

import jax
import jax.numpy as jnp
from jax import lax
from jax.experimental import pallas as pl
from jax.experimental.pallas import tpu as pltpu
from jax.sharding import PartitionSpec as P

alpha_fair = 0.95
absent = -1e30
steep = 3e38

BF = jnp.bfloat16
F32 = jnp.float32
I32 = jnp.int32
LANES = 128
CHUNK = 32
GX, GZ = 4, 8


def dot(a, b, ca=1, cb=0):
    return lax.dot_general(a, b, (((ca,), (cb,)), ((), ())), preferred_element_type=F32)


def iota(shape, dim):
    return lax.broadcasted_iota(I32, shape, dim)


def lane_gather(x, idx):
    dims = lax.GatherDimensionNumbers(
        offset_dims=(),
        collapsed_slice_dims=(1,),
        start_index_map=(1,),
        operand_batching_dims=(0,),
        start_indices_batching_dims=(0,),
    )
    return lax.gather(
        x, idx[..., None], dims, (1, 1), mode=lax.GatherScatterMode.PROMISE_IN_BOUNDS
    )


def fair_coefficient(member_count):
    return alpha_fair / (2.0 * member_count * (member_count - 1)) + (1.0 - alpha_fair) / (
        2.0 * member_count * member_count
    )


def wait_bytes(ref, sem):
    pltpu.make_async_copy(ref, ref, sem).wait()


def kernel(
    grid_count,
    member_count,
    pred_h, truth_h, area_h, q_h, cot_h, es_h, ec_h, eb_h, sr_h, we_h, wq_h, wkv_h, wo_h,
    hid_o, base_o, recve, sel, loss_o,
    predl, truth, area, q, cot, es_t, ec, eb, sr, we, wq, wkv, wo,
    pred, predp, wep, sendx, recvx, sende, crecv, csend, cret, lsend, lrecv,
    bias, qb, qst, ast, ww, qw, qw_t, aw, aw_t, values, s_scr, g_scr, gs_scr, wts, att,
    ld_sem, own_sem, fs, fr, cs, cr, rs, rr, ls, lr, bs, br, ws, wr, qs, qr,
):
    G, M = grid_count, member_count
    gi = lax.axis_index("grid")
    mi = lax.axis_index("member")
    variables, points = pred.shape
    nodes, width = q.shape
    pairs = width // LANES
    slots = sendx.shape[0]
    cap = slots // G
    fan = es_t.shape[0]
    coefficient = fair_coefficient(M)

    core = lax.rem(mi, 2)
    partner = mi + 1 - 2 * core
    wq_h = wq_h.at[:, pl.ds(pl.multiple_of(core * (width // 2), LANES), width // 2)]
    wkv_h = wkv_h.at[:, pl.ds(pl.multiple_of(core * width, LANES), width)]
    sources = [sr_h, pred_h, area_h, we_h, es_h, ec_h, eb_h, wkv_h, q_h, wq_h, cot_h, wo_h, truth_h]
    targets = [sr, predl, area, we, es_t, ec, eb, wkv, q, wq, cot, wo, truth]
    loads = [
        pltpu.make_async_copy(s, t, ld_sem.at[i]) for i, (s, t) in enumerate(zip(sources, targets))
    ]
    for c in loads[:4]:
        c.start()

    barrier = pltpu.get_barrier_semaphore()

    def turn(index, k, count):
        moved = index + k
        return jnp.where(moved >= count, moved - count, moved)

    gx, gz = lax.div(gi, GZ), lax.rem(gi, GZ)
    steps = [(dx, dz) for dx in range(GX) for dz in range(GZ)][1:]
    steps.sort(key=lambda d: -(min(d[0], GX - d[0]) + min(d[1], GZ - d[1])))
    tiles = [turn(gx, dx, GX) * GZ + turn(gz, dz, GZ) for dx, dz in steps]
    for peer in tiles:
        pl.semaphore_signal(barrier, inc=1, device_id={"grid": peer})
    for k in range(1, M):
        pl.semaphore_signal(barrier, inc=1, device_id={"member": turn(mi, k, M)})
    for c in loads[4:]:
        c.start()

    loads[0].wait()
    spots = jnp.broadcast_to(sr[0].astype(F32)[None], (G, cap, G)).reshape(slots, G)
    pick = iota((slots, G), 1) == (iota((slots, G), 0) // cap)
    rows = jnp.sum(jnp.where(pick, spots, 0.0), axis=1, keepdims=True).astype(I32)
    for c in range(slots // 64):
        r = pl.ds(64 * c, 64)
        hit = iota((64, points), 1) == rows[64 * c : 64 * c + 64]
        sel[r, :] = jnp.where(hit, 1.0, 0.0).astype(BF)
    predp[...] = jnp.zeros_like(predp)
    wep[...] = jnp.zeros_like(wep)
    for c in loads[1:4]:
        c.wait()
    pred[...] = predl[:, 0, :]
    pl.semaphore_wait(barrier, G - 1 + M - 1)
    for k in range(1, M):
        peer = turn(mi, k, M)
        pltpu.make_async_remote_copy(
            src_ref=pred.at[:, pl.ds(pl.multiple_of(peer * LANES, LANES), LANES)],
            dst_ref=crecv.at[mi],
            send_sem=cs,
            recv_sem=cr,
            device_id={"member": peer},
        ).start()
    own_lanes = pl.ds(pl.multiple_of(mi * LANES, LANES), LANES)
    own_chunk = pltpu.make_async_copy(pred.at[:, own_lanes], crecv.at[mi], own_sem)
    own_chunk.start()
    predp[0:variables, :] = pred[...].astype(BF)
    tile_area = jnp.sum(area[...], axis=1, keepdims=True)
    lane = iota((slots, LANES), 1)
    sub = iota((slots, LANES), 0)
    x = dot(sel[...], predp[...], 1, 1)
    sendx[...] = jnp.where(lane == variables, tile_area, x)


    mine = pl.ds(pl.multiple_of(gi * cap, cap), cap)

    def send_grid(src, dst, s_sem, r_sem):
        for peer in tiles:
            theirs = pl.ds(pl.multiple_of(peer * cap, cap), cap)
            pltpu.make_async_remote_copy(
                src_ref=src.at[theirs],
                dst_ref=dst.at[mine],
                send_sem=s_sem,
                recv_sem=r_sem,
                device_id={"grid": peer},
            ).start()
        dst[mine, :] = src[mine, :]

    send_grid(sendx, recvx, fs, fr)

    for c in loads[4:]:
        c.wait()
    wep[0:variables, :] = we[...]
    real = iota((fan, nodes), 0) < ec[...]
    es = jnp.where(real, es_t[...], -1).astype(F32).T.astype(I32)

    def spread_bias(start):
        r = slice(start, start + CHUNK)
        edges = es[r, :]
        slot_ids = iota((CHUNK, slots), 1)
        inverse = jnp.full((CHUNK, slots), -1, I32)
        for e in range(fan):
            inverse = jnp.where(edges[:, e : e + 1] == slot_ids, e, inverse)
        there = inverse >= 0
        index = jnp.maximum(inverse, 0)
        columns = [eb[r, j * LANES : (j + 1) * LANES] for j in range(4)]
        l = iota((CHUNK, LANES), 1)
        edge = l & (fan - 1)
        for t in range(4):
            place = (edge & 7) * 16 + 4 * t + (l >> 5)
            table = lane_gather(columns[0], place)
            for j in range(1, 4):
                table = jnp.where((edge >> 3) == j, lane_gather(columns[j], place), table)
            for hh in range(4):
                h = 4 * t + hh
                rows_of = slice((h % 2) * nodes + start, (h % 2) * nodes + start + CHUNK)
                for side in range(slots // LANES):
                    cols = slice(side * LANES, (side + 1) * LANES)
                    got = lane_gather(table, index[:, cols] + 32 * hh)
                    bias[h // 2, rows_of, cols] = jnp.where(there[:, cols], got, absent)

    half = LANES // 2
    for stacked in (qst, ast):
        stacked[...] = jnp.zeros_like(stacked)

    def stack_heads(p, block, stacked):
        stacked[p, 0:nodes, 0:half] = block[:, 0:half]
        stacked[p, nodes:, half:] = block[:, half:]

    def hand_over(ref, s_sem, r_sem):
        return pltpu.make_async_remote_copy(
            src_ref=ref.at[core],
            dst_ref=ref.at[core],
            send_sem=s_sem,
            recv_sem=r_sem,
            device_id={"member": partner},
        )

    spread_bias(0)
    for c in range(width // 512):
        cols = slice(512 * c, 512 * c + 512)
        ww[core, :, cols] = dot(wep[...], wkv[:, cols]).astype(BF)
    hand_over(ww, ws, wr).start()
    spread_bias(CHUNK)
    qb[core] = (dot(q[...], wq[...]) * 0.125).astype(BF)
    hand_over(qb, qs, qr).start()
    for c in range(width // 512):
        cols = slice(512 * c, 512 * c + 512)
        grads = dot(cot[0], wo[cols, :], 1, 1).astype(BF)
        spread_bias((2 + c) * CHUNK)
        for k in range(4):
            stack_heads(4 * c + k, grads[:, k * LANES : (k + 1) * LANES], ast)
    wait_bytes(qb.at[0], qr)
    wait_bytes(ww.at[0], wr)
    for p in range(pairs):
        lanes = slice(p * LANES, (p + 1) * LANES)
        inner = slice((p % 4) * LANES, (p % 4 + 1) * LANES)
        stack_heads(p, qb[p // 4, :, inner], qst)
        for stacked, weights, by_node, by_field in (
            (qst, ww[0, :, lanes], qw, qw_t),
            (ast, ww[1, :, lanes], aw, aw_t),
        ):
            by_node[p] = dot(stacked[p], weights, 1, 1).astype(BF)
            by_field[p] = dot(weights, stacked[p], 1, 1).astype(BF)

    wait_bytes(recvx.at[pl.ds(0, slots - cap)], fr)
    received = recvx[...]
    first = (lane == variables) & ((sub & (cap - 1)) == 0)
    total_area = jnp.sum(
        jnp.sum(jnp.where(first, received, 0.0), axis=0, keepdims=True), axis=1, keepdims=True
    )
    fields_t = received.T.astype(BF)

    def products(p):
        s_scr[p] = dot(qw[p], fields_t)
        g_scr[p] = dot(aw[p], fields_t)

    enc = jnp.zeros((LANES, slots), F32)
    def statistics():
        own_chunk.wait()
        wait_bytes(crecv.at[pl.ds(0, M - 1)], cr)

        own_area = area[:, own_lanes]
        part = jnp.zeros((1, LANES), F32)
        csend[:, variables // 16 * 16 :, :] = jnp.zeros((M, 16, LANES), BF)
        for row in range(0, variables, 16):
            r = slice(row, min(row + 16, variables))
            fields = [crecv[j, r, :] for j in range(M)]
            fact = truth[r, own_lanes]
            ranks = [jnp.zeros_like(fact) for _ in range(M)]
            skill = jnp.zeros_like(fact)
            for j in range(M):
                skill += jnp.abs(fields[j] - fact)
                for k in range(j + 1, M):
                    s = jnp.clip((fields[j] - fields[k]) * steep, -1.0, 1.0)
                    ranks[j] += s
                    ranks[k] -= s
            spread = sum(ranks[j] * fields[j] for j in range(M))
            crps = skill / M - (2.0 * coefficient) * spread
            part += jnp.sum(own_area * crps, axis=0, keepdims=True)
            for j in range(M):
                csend[j, r, :] = ranks[j].astype(BF)
        lsend[...] = jnp.broadcast_to(jnp.sum(part, axis=1, keepdims=True), lsend.shape)
        for k in range(1, M):
            pltpu.make_async_remote_copy(
                src_ref=lsend,
                dst_ref=lrecv.at[mi],
                send_sem=ls,
                recv_sem=lr,
                device_id={"member": turn(mi, k, M)},
            ).start()
        lrecv[mi] = lsend[...]
        for k in range(1, M):
            peer = turn(mi, k, M)
            pltpu.make_async_remote_copy(
                src_ref=csend.at[peer],
                dst_ref=cret.at[mi],
                send_sem=rs,
                recv_sem=rr,
                device_id={"member": peer},
            ).start()
        cret[mi] = csend[mi]

    products(0)
    for p in range(pairs):
        if p == 2:
            statistics()
        if p + 1 < pairs:
            products(p + 1)
        for i in range(2):
            r = slice(i * nodes, (i + 1) * nodes)
            s = s_scr[p, r, :] + bias[p, r, :]
            e = jnp.exp(s - jnp.max(s, axis=1, keepdims=True))
            g = g_scr[p, r, :]
            share = 1.0 / jnp.sum(e, axis=1, keepdims=True)
            inner = jnp.sum(e * g, axis=1, keepdims=True) * share
            w = e * share
            wts[p, r, :] = w.astype(BF)
            gs_scr[p, r, :] = (w * (g - inner)).astype(BF)
        enc += dot(qw_t[p], gs_scr[p]) + dot(aw_t[p], wts[p])

    wait_bytes(lrecv.at[pl.ds(0, M - 1)], lr)
    tile_loss = jnp.sum(lrecv[:, 0, 0:1], axis=0, keepdims=True)
    sende[...] = jnp.where(lane == variables, tile_loss, enc.T)
    send_grid(sende, recve, bs, br)

    low = iota((nodes, LANES), 1) < half
    values[...] = dot(recvx[...].astype(BF), ww[1]).astype(BF)
    for p in range(pairs):
        both = dot(wts[p], values[:, p * LANES : (p + 1) * LANES])
        att[:, p * LANES : (p + 1) * LANES] = jnp.where(low, both[:nodes], both[nodes:]).astype(BF)
    hid_o[0] = (q[...].astype(F32) + dot(att[...], wo[...])).astype(BF)

    wait_bytes(cret.at[pl.ds(0, M - 1)], rr)
    scale = (points * G) / total_area
    for chunk in range(points // LANES):
        cols = slice(chunk * LANES, (chunk + 1) * LANES)
        d = pred[:, cols] - truth[:, cols]
        s = jnp.where(d > 0, 1.0, jnp.where(d < 0, -1.0, 0.0)) / M
        slope = s - (2.0 * coefficient) * cret[chunk, 0:variables, :].astype(F32)
        base_o[:, cols] = (area[:, cols] * scale) * slope

    wait_bytes(recve.at[pl.ds(0, slots - cap)], br)
    back = recve[...]
    total_loss = jnp.sum(
        jnp.sum(jnp.where(first, back, 0.0), axis=0, keepdims=True), axis=1, keepdims=True
    )
    loss_o[...] = total_loss / (total_area * variables)
    wait_bytes(sendx.at[pl.ds(0, slots - cap)], fs)
    wait_bytes(sende.at[pl.ds(0, slots - cap)], bs)
    wait_bytes(crecv.at[pl.ds(0, M - 1)], cs)
    wait_bytes(csend.at[pl.ds(0, M - 1)], rs)
    wait_bytes(lrecv.at[pl.ds(0, M - 1)], ls)
    wait_bytes(ww.at[0], ws)
    wait_bytes(qb.at[0], qs)


def finish(hid, base, recve, sel, loss, hid_o, grad_o, loss_o, grad, sems):
    variables, points = base.shape
    copies = [
        pltpu.make_async_copy(hid, hid_o, sems.at[0]),
        pltpu.make_async_copy(loss, loss_o, sems.at[1]),
    ]
    for c in copies:
        c.start()
    back = recve[...].T
    high = back.astype(BF)
    terms = jnp.concatenate([high, (back - high.astype(F32)).astype(BF)], axis=0)
    for c in range(points // 512):
        cols = slice(512 * c, 512 * c + 512)
        both = dot(terms, sel[:, cols])
        grad[:, 0, cols] = base[:, cols] + (both[:LANES] + both[LANES:])[:variables]
        copy = pltpu.make_async_copy(grad.at[:, :, cols], grad_o.at[:, :, cols], sems.at[2 + c])
        copy.start()
        copies.append(copy)
    for c in copies:
        c.wait()


def local(
    grid_count, member_count,
    predictions, truth, area, queries, cotangent, edge_slot, edge_count, edge_bias, send_rows,
    w_embed, w_query, w_keyval, w_out,
):
    G, M = grid_count, member_count
    variables, points = truth.shape
    nodes, width = queries.shape
    slots = send_rows.shape[1] * send_rows.shape[2]
    pairs = width // LANES
    area = area.reshape(1, points)
    edge_count = edge_count.reshape(1, nodes)
    predictions = jnp.transpose(predictions, (1, 0, 2))
    edge_slot = edge_slot.T
    send_rows = jnp.transpose(send_rows, (0, 2, 1))
    args = (
        predictions, truth, area, queries, cotangent, edge_slot, edge_count, edge_bias, send_rows,
        w_embed, w_query, w_keyval, w_out,
    )
    args = tuple(pltpu.with_memory_space_constraint(a, pltpu.HBM) for a in args)
    rank_rows = (variables + 15) // 16 * 16
    hbm_spec = pl.BlockSpec(memory_space=pltpu.HBM)
    vmem_spec = pl.BlockSpec(memory_space=pltpu.VMEM)
    vm = pltpu.VMEM
    dma = pltpu.SemaphoreType.DMA
    shapes = [a.shape for a in args]
    shapes[10] = (width, width // 2)
    shapes[11] = (width, width)
    parts = pl.pallas_call(
        functools.partial(kernel, G, M),
        out_shape=(
            vm((1, nodes, width), BF),
            vm((variables, points), F32),
            vm((slots, LANES), F32),
            vm((slots, points), BF),
            vm((1, 1), F32),
        ),
        in_specs=[hbm_spec] * len(args),
        out_specs=(vmem_spec,) * 5,
        scratch_shapes=[vm(shape, a.dtype) for shape, a in zip(shapes, args)]
        + [
            vm((variables, points), F32),
            vm((LANES, points), BF),
            vm((LANES, width), BF),
            vm((slots, LANES), F32),
            vm((slots, LANES), F32),
            vm((slots, LANES), F32),
            vm((M, variables, LANES), F32),
            vm((M, rank_rows, LANES), BF),
            vm((M, rank_rows, LANES), BF),
            vm((8, LANES), F32),
            vm((M, 8, LANES), F32),
            vm((pairs, 2 * nodes, slots), F32),
            vm((2, nodes, width // 2), BF),
            vm((pairs, 2 * nodes, LANES), BF),
            vm((pairs, 2 * nodes, LANES), BF),
            vm((2, LANES, width), BF),
            vm((pairs, 2 * nodes, LANES), BF),
            vm((pairs, LANES, 2 * nodes), BF),
            vm((pairs, 2 * nodes, LANES), BF),
            vm((pairs, LANES, 2 * nodes), BF),
            vm((slots, width), BF),
            vm((pairs, 2 * nodes, slots), F32),
            vm((pairs, 2 * nodes, slots), F32),
            vm((pairs, 2 * nodes, slots), BF),
            vm((pairs, 2 * nodes, slots), BF),
            vm((nodes, width), BF),
            dma((len(args),)),
            *([dma] * 15),
        ],
        compiler_params=pltpu.CompilerParams(
            collective_id=0, has_side_effects=True, vmem_limit_bytes=48 * 1024 * 1024
        ),
    )(*args)
    hidden, grad_pred, loss = pl.pallas_call(
        finish,
        out_shape=(
            jax.ShapeDtypeStruct((1, nodes, width), BF),
            jax.ShapeDtypeStruct((variables, 1, points), F32),
            jax.ShapeDtypeStruct((1, 1), F32),
        ),
        in_specs=[vmem_spec] * 5,
        out_specs=(hbm_spec,) * 3,
        scratch_shapes=[vm((variables, 1, points), F32), dma((4,))],
        compiler_params=pltpu.CompilerParams(vmem_limit_bytes=16 * 1024 * 1024),
    )(*parts)
    return hidden, jnp.transpose(grad_pred, (1, 0, 2)), loss.reshape(())


def solution(mesh):
    return jax.shard_map(
        functools.partial(local, mesh.shape["grid"], mesh.shape["member"]),
        mesh=mesh,
        in_specs=(
            P("member", None, "grid"),
            P(None, "grid"),
            P("grid"),
            P("grid", None),
            P("member", "grid", None),
            P("grid", None),
            P("grid"),
            P("grid", None),
            P("grid", None, None),
            P(),
            P(),
            P(),
            P(),
        ),
        out_specs=(P("member", "grid", None), P("member", None, "grid"), P()),
        check_vma=False,
    )
```

```python
import functools

import jax
import jax.numpy as jnp
from jax import lax
from jax.experimental import pallas as pl
from jax.experimental.pallas import tpu as pltpu
from jax.sharding import PartitionSpec as P

alpha_fair = 0.95
absent = -1e30
steep = 3e38

BF = jnp.bfloat16
F32 = jnp.float32
I32 = jnp.int32
LANES = 128
CHUNK = 32
GX, GZ = 4, 8


def dot(a, b, ca=1, cb=0):
    return lax.dot_general(a, b, (((ca,), (cb,)), ((), ())), preferred_element_type=F32)


def iota(shape, dim):
    return lax.broadcasted_iota(I32, shape, dim)


def lane_gather(x, idx):
    dims = lax.GatherDimensionNumbers(
        offset_dims=(),
        collapsed_slice_dims=(1,),
        start_index_map=(1,),
        operand_batching_dims=(0,),
        start_indices_batching_dims=(0,),
    )
    return lax.gather(
        x, idx[..., None], dims, (1, 1), mode=lax.GatherScatterMode.PROMISE_IN_BOUNDS
    )


def fair_coefficient(member_count):
    return alpha_fair / (2.0 * member_count * (member_count - 1)) + (1.0 - alpha_fair) / (
        2.0 * member_count * member_count
    )


def wait_bytes(ref, sem):
    pltpu.make_async_copy(ref, ref, sem).wait()


def kernel(
    grid_count,
    member_count,
    pred_h, truth_h, area_h, q_h, cot_h, es_h, ec_h, eb_h, sr_h, we_h, wq_h, wkv_h, wo_h,
    hid_o, base_o, recve, sel, area_o,
    predl, truth, area, q, cot, es_t, ec, eb, sr, we, wq, wkv, wo,
    pred, predp, wep, sendx, recvx, sende, crecv, csend, cret, lsend, lrecv,
    bias, qb, qst, ast, ww, qw, qw_t, aw, aw_t, values, s_scr, g_scr, gs_scr, wts, att,
    ld_sem, own_sem, fs, fr, cs, cr, rs, rr, ls, lr, bs, br, ws, wr, qs, qr,
):
    G, M = grid_count, member_count
    gi = lax.axis_index("grid")
    mi = lax.axis_index("member")
    variables, points = pred.shape
    nodes, width = q.shape
    pairs = width // LANES
    slots = sendx.shape[0]
    cap = slots // G
    fan = es_t.shape[0]
    coefficient = fair_coefficient(M)

    core = lax.rem(mi, 2)
    partner = mi + 1 - 2 * core
    wq_h = wq_h.at[:, pl.ds(pl.multiple_of(core * (width // 2), LANES), width // 2)]
    wkv_h = wkv_h.at[:, pl.ds(pl.multiple_of(core * width, LANES), width)]
    sources = [sr_h, pred_h, area_h, we_h, wkv_h, q_h, wq_h, es_h, ec_h, eb_h, cot_h, wo_h, truth_h]
    targets = [sr, predl, area, we, wkv, q, wq, es_t, ec, eb, cot, wo, truth]
    loads = [
        pltpu.make_async_copy(s, t, ld_sem.at[i]) for i, (s, t) in enumerate(zip(sources, targets))
    ]
    for c in loads[:4]:
        c.start()

    barrier = pltpu.get_barrier_semaphore()

    def turn(index, k, count):
        moved = index + k
        return jnp.where(moved >= count, moved - count, moved)

    gx, gz = lax.div(gi, GZ), lax.rem(gi, GZ)
    steps = [(dx, dz) for dx in range(GX) for dz in range(GZ)][1:]
    steps.sort(key=lambda d: -(min(d[0], GX - d[0]) + min(d[1], GZ - d[1])))
    tiles = [turn(gx, dx, GX) * GZ + turn(gz, dz, GZ) for dx, dz in steps]
    for peer in tiles:
        pl.semaphore_signal(barrier, inc=1, device_id={"grid": peer})
    for k in range(1, M):
        pl.semaphore_signal(barrier, inc=1, device_id={"member": turn(mi, k, M)})
    for c in loads[4:]:
        c.start()

    loads[0].wait()
    spots = jnp.broadcast_to(sr[0].astype(F32)[None], (G, cap, G)).reshape(slots, G)
    pick = iota((slots, G), 1) == (iota((slots, G), 0) // cap)
    rows = jnp.sum(jnp.where(pick, spots, 0.0), axis=1, keepdims=True).astype(I32)
    for c in range(slots // 64):
        r = pl.ds(64 * c, 64)
        hit = iota((64, points), 1) == rows[64 * c : 64 * c + 64]
        sel[r, :] = jnp.where(hit, 1.0, 0.0).astype(BF)
    predp[...] = jnp.zeros_like(predp)
    wep[...] = jnp.zeros_like(wep)
    for c in loads[1:4]:
        c.wait()
    pred[...] = predl[:, 0, :]
    predp[0:variables, :] = pred[...].astype(BF)
    tile_area = jnp.sum(area[...], axis=1, keepdims=True)
    lane = iota((slots, LANES), 1)
    sub = iota((slots, LANES), 0)
    x = dot(sel[...], predp[...], 1, 1)
    sendx[...] = jnp.where(lane == variables, tile_area, x)


    for c in loads[4:7]:
        c.wait()
    wep[0:variables, :] = we[...]
    for c in range(width // 512):
        cols = slice(512 * c, 512 * c + 512)
        ww[core, :, cols] = dot(wep[...], wkv[:, cols]).astype(BF)
    qb[core] = (dot(q[...], wq[...]) * 0.125).astype(BF)

    pl.semaphore_wait(barrier, G - 1 + M - 1)

    def hand_over(ref, s_sem, r_sem):
        return pltpu.make_async_remote_copy(
            src_ref=ref.at[core],
            dst_ref=ref.at[core],
            send_sem=s_sem,
            recv_sem=r_sem,
            device_id={"member": partner},
        )

    hand_over(ww, ws, wr).start()
    hand_over(qb, qs, qr).start()

    mine = pl.ds(pl.multiple_of(gi * cap, cap), cap)

    def send_grid(src, dst, s_sem, r_sem):
        for peer in tiles:
            theirs = pl.ds(pl.multiple_of(peer * cap, cap), cap)
            pltpu.make_async_remote_copy(
                src_ref=src.at[theirs],
                dst_ref=dst.at[mine],
                send_sem=s_sem,
                recv_sem=r_sem,
                device_id={"grid": peer},
            ).start()
        dst[mine, :] = src[mine, :]

    send_grid(sendx, recvx, fs, fr)

    for k in range(1, M):
        peer = turn(mi, k, M)
        pltpu.make_async_remote_copy(
            src_ref=pred.at[:, pl.ds(pl.multiple_of(peer * LANES, LANES), LANES)],
            dst_ref=crecv.at[mi],
            send_sem=cs,
            recv_sem=cr,
            device_id={"member": peer},
        ).start()
    own_lanes = pl.ds(pl.multiple_of(mi * LANES, LANES), LANES)
    own_chunk = pltpu.make_async_copy(pred.at[:, own_lanes], crecv.at[mi], own_sem)
    own_chunk.start()

    for c in loads[7:]:
        c.wait()
    real = iota((fan, nodes), 0) < ec[...]
    es = jnp.where(real, es_t[...], -1).astype(F32).T.astype(I32)

    def spread_bias(start):
        r = slice(start, start + CHUNK)
        edges = es[r, :]
        slot_ids = iota((CHUNK, slots), 1)
        inverse = jnp.full((CHUNK, slots), -1, I32)
        for e in range(fan):
            inverse = jnp.where(edges[:, e : e + 1] == slot_ids, e, inverse)
        there = inverse >= 0
        index = jnp.maximum(inverse, 0)
        columns = [eb[r, j * LANES : (j + 1) * LANES] for j in range(4)]
        l = iota((CHUNK, LANES), 1)
        edge = l & (fan - 1)
        for t in range(4):
            place = (edge & 7) * 16 + 4 * t + (l >> 5)
            table = lane_gather(columns[0], place)
            for j in range(1, 4):
                table = jnp.where((edge >> 3) == j, lane_gather(columns[j], place), table)
            for hh in range(4):
                h = 4 * t + hh
                rows_of = slice((h % 2) * nodes + start, (h % 2) * nodes + start + CHUNK)
                for side in range(slots // LANES):
                    cols = slice(side * LANES, (side + 1) * LANES)
                    got = lane_gather(table, index[:, cols] + 32 * hh)
                    bias[h // 2, rows_of, cols] = jnp.where(there[:, cols], got, absent)

    half = LANES // 2
    for stacked in (qst, ast):
        stacked[...] = jnp.zeros_like(stacked)

    def stack_heads(p, block, stacked):
        stacked[p, 0:nodes, 0:half] = block[:, 0:half]
        stacked[p, nodes:, half:] = block[:, half:]

    for c in range(width // 512):
        cols = slice(512 * c, 512 * c + 512)
        grads = dot(cot[0], wo[cols, :], 1, 1).astype(BF)
        spread_bias(2 * c * CHUNK)
        spread_bias((2 * c + 1) * CHUNK)
        for k in range(4):
            stack_heads(4 * c + k, grads[:, k * LANES : (k + 1) * LANES], ast)
    wait_bytes(qb.at[0], qr)
    wait_bytes(ww.at[0], wr)
    for p in range(pairs):
        lanes = slice(p * LANES, (p + 1) * LANES)
        inner = slice((p % 4) * LANES, (p % 4 + 1) * LANES)
        stack_heads(p, qb[p // 4, :, inner], qst)
        for stacked, weights, by_node, by_field in (
            (qst, ww[0, :, lanes], qw, qw_t),
            (ast, ww[1, :, lanes], aw, aw_t),
        ):
            by_node[p] = dot(stacked[p], weights, 1, 1).astype(BF)
            by_field[p] = dot(weights, stacked[p], 1, 1).astype(BF)

    wait_bytes(recvx.at[pl.ds(0, slots - cap)], fr)
    received = recvx[...]
    first = (lane == variables) & ((sub & (cap - 1)) == 0)
    total_area = jnp.sum(
        jnp.sum(jnp.where(first, received, 0.0), axis=0, keepdims=True), axis=1, keepdims=True
    )
    fields_t = received.T.astype(BF)

    def products(p):
        s_scr[p] = dot(qw[p], fields_t)
        g_scr[p] = dot(aw[p], fields_t)

    enc = jnp.zeros((LANES, slots), F32)
    def statistics():
        own_chunk.wait()
        wait_bytes(crecv.at[pl.ds(0, M - 1)], cr)

        own_area = area[:, own_lanes]
        part = jnp.zeros((1, LANES), F32)
        csend[:, variables // 16 * 16 :, :] = jnp.zeros((M, 16, LANES), BF)
        for row in range(0, variables, 16):
            r = slice(row, min(row + 16, variables))
            fields = [crecv[j, r, :] for j in range(M)]
            fact = truth[r, own_lanes]
            ranks = [jnp.zeros_like(fact) for _ in range(M)]
            skill = jnp.zeros_like(fact)
            for j in range(M):
                skill += jnp.abs(fields[j] - fact)
                for k in range(j + 1, M):
                    s = jnp.clip((fields[j] - fields[k]) * steep, -1.0, 1.0)
                    ranks[j] += s
                    ranks[k] -= s
            spread = sum(ranks[j] * fields[j] for j in range(M))
            crps = skill / M - (2.0 * coefficient) * spread
            part += jnp.sum(own_area * crps, axis=0, keepdims=True)
            for j in range(M):
                csend[j, r, :] = ranks[j].astype(BF)
        lsend[...] = jnp.broadcast_to(jnp.sum(part, axis=1, keepdims=True), lsend.shape)
        for k in range(1, M):
            pltpu.make_async_remote_copy(
                src_ref=lsend,
                dst_ref=lrecv.at[mi],
                send_sem=ls,
                recv_sem=lr,
                device_id={"member": turn(mi, k, M)},
            ).start()
        lrecv[mi] = lsend[...]
        for k in range(1, M):
            peer = turn(mi, k, M)
            pltpu.make_async_remote_copy(
                src_ref=csend.at[peer],
                dst_ref=cret.at[mi],
                send_sem=rs,
                recv_sem=rr,
                device_id={"member": peer},
            ).start()
        cret[mi] = csend[mi]

    products(0)
    for p in range(pairs):
        if p == 5:
            statistics()
        if p + 1 < pairs:
            products(p + 1)
        for i in range(2):
            r = slice(i * nodes, (i + 1) * nodes)
            s = s_scr[p, r, :] + bias[p, r, :]
            e = jnp.exp(s - jnp.max(s, axis=1, keepdims=True))
            g = g_scr[p, r, :]
            share = 1.0 / jnp.sum(e, axis=1, keepdims=True)
            inner = jnp.sum(e * g, axis=1, keepdims=True) * share
            w = e * share
            wts[p, r, :] = w.astype(BF)
            gs_scr[p, r, :] = (w * (g - inner)).astype(BF)
        enc += dot(qw_t[p], gs_scr[p]) + dot(aw_t[p], wts[p])

    wait_bytes(lrecv.at[pl.ds(0, M - 1)], lr)
    tile_loss = jnp.sum(lrecv[:, 0, 0:1], axis=0, keepdims=True)
    sende[...] = jnp.where(lane == variables, tile_loss, enc.T)
    send_grid(sende, recve, bs, br)

    low = iota((nodes, LANES), 1) < half
    values[...] = dot(recvx[...].astype(BF), ww[1]).astype(BF)
    for p in range(pairs):
        both = dot(wts[p], values[:, p * LANES : (p + 1) * LANES])
        att[:, p * LANES : (p + 1) * LANES] = jnp.where(low, both[:nodes], both[nodes:]).astype(BF)
    hid_o[0] = (q[...].astype(F32) + dot(att[...], wo[...])).astype(BF)

    wait_bytes(cret.at[pl.ds(0, M - 1)], rr)
    area_o[...] = total_area
    scale = (points * G) / total_area
    for chunk in range(points // LANES):
        cols = slice(chunk * LANES, (chunk + 1) * LANES)
        d = pred[:, cols] - truth[:, cols]
        s = jnp.where(d > 0, 1.0, jnp.where(d < 0, -1.0, 0.0)) / M
        slope = s - (2.0 * coefficient) * cret[chunk, 0:variables, :].astype(F32)
        base_o[:, cols] = (area[:, cols] * scale) * slope

    wait_bytes(recve.at[pl.ds(0, slots - cap)], br)
    wait_bytes(sendx.at[pl.ds(0, slots - cap)], fs)
    wait_bytes(sende.at[pl.ds(0, slots - cap)], bs)
    wait_bytes(crecv.at[pl.ds(0, M - 1)], cs)
    wait_bytes(csend.at[pl.ds(0, M - 1)], rs)
    wait_bytes(lrecv.at[pl.ds(0, M - 1)], ls)
    wait_bytes(ww.at[0], ws)
    wait_bytes(qb.at[0], qs)


def finish(cap, hid, base, recve, sel, area, hid_o, grad_o, loss_o, grad, loss, sems):
    variables, points = base.shape
    copies = [pltpu.make_async_copy(hid, hid_o, sems.at[0])]
    copies[0].start()
    back = recve[...].T
    high = back.astype(BF)
    terms = jnp.concatenate([high, (back - high.astype(F32)).astype(BF)], axis=0)
    for c in range(points // 512):
        cols = slice(512 * c, 512 * c + 512)
        both = dot(terms, sel[:, cols])
        grad[:, 0, cols] = base[:, cols] + (both[:LANES] + both[LANES:])[:variables]
        copy = pltpu.make_async_copy(grad.at[:, :, cols], grad_o.at[:, :, cols], sems.at[2 + c])
        copy.start()
        copies.append(copy)
    back = recve[...]
    first = (iota(back.shape, 1) == variables) & ((iota(back.shape, 0) & (cap - 1)) == 0)
    total = jnp.sum(jnp.where(first, back, 0.0), axis=0, keepdims=True)
    loss[...] = jnp.sum(total, axis=1, keepdims=True) / (area[...] * variables)
    copy = pltpu.make_async_copy(loss, loss_o, sems.at[1])
    copy.start()
    for c in copies + [copy]:
        c.wait()


def local(
    grid_count, member_count,
    predictions, truth, area, queries, cotangent, edge_slot, edge_count, edge_bias, send_rows,
    w_embed, w_query, w_keyval, w_out,
):
    G, M = grid_count, member_count
    variables, points = truth.shape
    nodes, width = queries.shape
    slots = send_rows.shape[1] * send_rows.shape[2]
    pairs = width // LANES
    area = area.reshape(1, points)
    edge_count = edge_count.reshape(1, nodes)
    predictions = jnp.transpose(predictions, (1, 0, 2))
    edge_slot = edge_slot.T
    send_rows = jnp.transpose(send_rows, (0, 2, 1))
    args = (
        predictions, truth, area, queries, cotangent, edge_slot, edge_count, edge_bias, send_rows,
        w_embed, w_query, w_keyval, w_out,
    )
    args = tuple(pltpu.with_memory_space_constraint(a, pltpu.HBM) for a in args)
    rank_rows = (variables + 15) // 16 * 16
    hbm_spec = pl.BlockSpec(memory_space=pltpu.HBM)
    vmem_spec = pl.BlockSpec(memory_space=pltpu.VMEM)
    vm = pltpu.VMEM
    dma = pltpu.SemaphoreType.DMA
    shapes = [a.shape for a in args]
    shapes[10] = (width, width // 2)
    shapes[11] = (width, width)
    parts = pl.pallas_call(
        functools.partial(kernel, G, M),
        out_shape=(
            vm((1, nodes, width), BF),
            vm((variables, points), F32),
            vm((slots, LANES), F32),
            vm((slots, points), BF),
            vm((1, 1), F32),
        ),
        in_specs=[hbm_spec] * len(args),
        out_specs=(vmem_spec,) * 5,
        scratch_shapes=[vm(shape, a.dtype) for shape, a in zip(shapes, args)]
        + [
            vm((variables, points), F32),
            vm((LANES, points), BF),
            vm((LANES, width), BF),
            vm((slots, LANES), F32),
            vm((slots, LANES), F32),
            vm((slots, LANES), F32),
            vm((M, variables, LANES), F32),
            vm((M, rank_rows, LANES), BF),
            vm((M, rank_rows, LANES), BF),
            vm((8, LANES), F32),
            vm((M, 8, LANES), F32),
            vm((pairs, 2 * nodes, slots), F32),
            vm((2, nodes, width // 2), BF),
            vm((pairs, 2 * nodes, LANES), BF),
            vm((pairs, 2 * nodes, LANES), BF),
            vm((2, LANES, width), BF),
            vm((pairs, 2 * nodes, LANES), BF),
            vm((pairs, LANES, 2 * nodes), BF),
            vm((pairs, 2 * nodes, LANES), BF),
            vm((pairs, LANES, 2 * nodes), BF),
            vm((slots, width), BF),
            vm((pairs, 2 * nodes, slots), F32),
            vm((pairs, 2 * nodes, slots), F32),
            vm((pairs, 2 * nodes, slots), BF),
            vm((pairs, 2 * nodes, slots), BF),
            vm((nodes, width), BF),
            dma((len(args),)),
            *([dma] * 15),
        ],
        compiler_params=pltpu.CompilerParams(
            collective_id=0, has_side_effects=True, vmem_limit_bytes=48 * 1024 * 1024
        ),
    )(*args)
    hidden, grad_pred, loss = pl.pallas_call(
        functools.partial(finish, slots // G),
        out_shape=(
            jax.ShapeDtypeStruct((1, nodes, width), BF),
            jax.ShapeDtypeStruct((variables, 1, points), F32),
            jax.ShapeDtypeStruct((1, 1), F32),
        ),
        in_specs=[vmem_spec] * 5,
        out_specs=(hbm_spec,) * 3,
        scratch_shapes=[vm((variables, 1, points), F32), vm((1, 1), F32), dma((4,))],
        compiler_params=pltpu.CompilerParams(vmem_limit_bytes=16 * 1024 * 1024),
    )(*parts)
    return hidden, jnp.transpose(grad_pred, (1, 0, 2)), loss.reshape(())


def solution(mesh):
    return jax.shard_map(
        functools.partial(local, mesh.shape["grid"], mesh.shape["member"]),
        mesh=mesh,
        in_specs=(
            P("member", None, "grid"),
            P(None, "grid"),
            P("grid"),
            P("grid", None),
            P("member", "grid", None),
            P("grid", None),
            P("grid"),
            P("grid", None),
            P("grid", None, None),
            P(),
            P(),
            P(),
            P(),
        ),
        out_specs=(P("member", "grid", None), P("member", None, "grid"), P()),
        check_vma=False,
    )
```

```python
import functools

import jax
import jax.numpy as jnp
from jax import lax
from jax.experimental import pallas as pl
from jax.experimental.pallas import tpu as pltpu
from jax.sharding import PartitionSpec as P

alpha_fair = 0.95
absent = -1e30
steep = 3e38

BF = jnp.bfloat16
F32 = jnp.float32
I32 = jnp.int32
LANES = 128
CHUNK = 32
GX, GZ = 4, 8


def dot(a, b, ca=1, cb=0):
    return lax.dot_general(a, b, (((ca,), (cb,)), ((), ())), preferred_element_type=F32)


def iota(shape, dim):
    return lax.broadcasted_iota(I32, shape, dim)


def lane_gather(x, idx):
    dims = lax.GatherDimensionNumbers(
        offset_dims=(),
        collapsed_slice_dims=(1,),
        start_index_map=(1,),
        operand_batching_dims=(0,),
        start_indices_batching_dims=(0,),
    )
    return lax.gather(
        x, idx[..., None], dims, (1, 1), mode=lax.GatherScatterMode.PROMISE_IN_BOUNDS
    )


def fair_coefficient(member_count):
    return alpha_fair / (2.0 * member_count * (member_count - 1)) + (1.0 - alpha_fair) / (
        2.0 * member_count * member_count
    )


def wait_bytes(ref, sem):
    pltpu.make_async_copy(ref, ref, sem).wait()


def kernel(
    grid_count,
    member_count,
    pred_h, truth_h, area_h, q_h, cot_h, es_h, ec_h, eb_h, sr_h, we_h, wq_h, wkv_h, wo_h,
    hid_o, base_o, recve, sel, area_o,
    predl, truth, area, q, cot, es_t, ec, eb, sr, we, wq, wkv, wo,
    pred, predp, wep, sendx, recvx, sende, crecv, csend, cret, lsend, lrecv,
    bias, qb, qst, ast, ww, qw, qw_t, aw, aw_t, values, s_scr, g_scr, gs_scr, wts, att,
    ld_sem, own_sem, fs, fr, cs, cr, rs, rr, ls, lr, bs, br, ws, wr, qs, qr,
):
    G, M = grid_count, member_count
    gi = lax.axis_index("grid")
    mi = lax.axis_index("member")
    variables, points = pred.shape
    nodes, width = q.shape
    pairs = width // LANES
    slots = sendx.shape[0]
    cap = slots // G
    fan = es_t.shape[0]
    coefficient = fair_coefficient(M)

    core = lax.rem(mi, 2)
    partner = mi + 1 - 2 * core
    wq_h = wq_h.at[:, pl.ds(pl.multiple_of(core * (width // 2), LANES), width // 2)]
    wkv_h = wkv_h.at[:, pl.ds(pl.multiple_of(core * width, LANES), width)]
    sources = [sr_h, pred_h, area_h, we_h, es_h, ec_h, eb_h, q_h, wkv_h, wq_h, cot_h, wo_h, truth_h]
    targets = [sr, predl, area, we, es_t, ec, eb, q, wkv, wq, cot, wo, truth]
    loads = [
        pltpu.make_async_copy(s, t, ld_sem.at[i]) for i, (s, t) in enumerate(zip(sources, targets))
    ]
    for c in loads[:4]:
        c.start()

    barrier = pltpu.get_barrier_semaphore()

    def turn(index, k, count):
        moved = index + k
        return jnp.where(moved >= count, moved - count, moved)

    gx, gz = lax.div(gi, GZ), lax.rem(gi, GZ)
    steps = [(dx, dz) for dx in range(GX) for dz in range(GZ)][1:]
    steps.sort(key=lambda d: -(min(d[0], GX - d[0]) + min(d[1], GZ - d[1])))
    tiles = [turn(gx, dx, GX) * GZ + turn(gz, dz, GZ) for dx, dz in steps]
    for peer in tiles:
        pl.semaphore_signal(barrier, inc=1, device_id={"grid": peer})
    for k in range(1, M):
        pl.semaphore_signal(barrier, inc=1, device_id={"member": turn(mi, k, M)})
    for c in loads[4:]:
        c.start()

    loads[0].wait()
    spots = jnp.broadcast_to(sr[0].astype(F32)[None], (G, cap, G)).reshape(slots, G)
    pick = iota((slots, G), 1) == (iota((slots, G), 0) // cap)
    rows = jnp.sum(jnp.where(pick, spots, 0.0), axis=1, keepdims=True).astype(I32)
    for c in range(slots // 64):
        r = pl.ds(64 * c, 64)
        hit = iota((64, points), 1) == rows[64 * c : 64 * c + 64]
        sel[r, :] = jnp.where(hit, 1.0, 0.0).astype(BF)
    predp[...] = jnp.zeros_like(predp)
    wep[...] = jnp.zeros_like(wep)
    for c in loads[1:10]:
        c.wait()
    wep[0:variables, :] = we[...]
    pred[...] = predl[:, 0, :]
    predp[0:variables, :] = pred[...].astype(BF)
    tile_area = jnp.sum(area[...], axis=1, keepdims=True)
    lane = iota((slots, LANES), 1)
    sub = iota((slots, LANES), 0)
    x = dot(sel[...], predp[...], 1, 1)
    sendx[...] = jnp.where(lane == variables, tile_area, x)


    real = iota((fan, nodes), 0) < ec[...]
    es = jnp.where(real, es_t[...], -1).astype(F32).T.astype(I32)

    def spread_bias(start):
        r = slice(start, start + CHUNK)
        edges = es[r, :]
        slot_ids = iota((CHUNK, slots), 1)
        inverse = jnp.full((CHUNK, slots), -1, I32)
        for e in range(fan):
            inverse = jnp.where(edges[:, e : e + 1] == slot_ids, e, inverse)
        there = inverse >= 0
        index = jnp.maximum(inverse, 0)
        columns = [eb[r, j * LANES : (j + 1) * LANES] for j in range(4)]
        l = iota((CHUNK, LANES), 1)
        edge = l & (fan - 1)
        for t in range(4):
            place = (edge & 7) * 16 + 4 * t + (l >> 5)
            table = lane_gather(columns[0], place)
            for j in range(1, 4):
                table = jnp.where((edge >> 3) == j, lane_gather(columns[j], place), table)
            for hh in range(4):
                h = 4 * t + hh
                rows_of = slice((h % 2) * nodes + start, (h % 2) * nodes + start + CHUNK)
                for side in range(slots // LANES):
                    cols = slice(side * LANES, (side + 1) * LANES)
                    got = lane_gather(table, index[:, cols] + 32 * hh)
                    bias[h // 2, rows_of, cols] = jnp.where(there[:, cols], got, absent)

    for c in range(width // 512):
        cols = slice(512 * c, 512 * c + 512)
        ww[core, :, cols] = dot(wep[...], wkv[:, cols]).astype(BF)
        spread_bias(c * CHUNK)
    qb[core] = (dot(q[...], wq[...]) * 0.125).astype(BF)
    for c in range(width // 512, nodes // CHUNK):
        spread_bias(c * CHUNK)

    for c in loads[10:]:
        c.wait()
    pl.semaphore_wait(barrier, G - 1 + M - 1)

    def hand_over(ref, s_sem, r_sem):
        return pltpu.make_async_remote_copy(
            src_ref=ref.at[core],
            dst_ref=ref.at[core],
            send_sem=s_sem,
            recv_sem=r_sem,
            device_id={"member": partner},
        )

    hand_over(ww, ws, wr).start()
    hand_over(qb, qs, qr).start()

    mine = pl.ds(pl.multiple_of(gi * cap, cap), cap)

    def send_grid(src, dst, s_sem, r_sem):
        for peer in tiles:
            theirs = pl.ds(pl.multiple_of(peer * cap, cap), cap)
            pltpu.make_async_remote_copy(
                src_ref=src.at[theirs],
                dst_ref=dst.at[mine],
                send_sem=s_sem,
                recv_sem=r_sem,
                device_id={"grid": peer},
            ).start()
        dst[mine, :] = src[mine, :]

    send_grid(sendx, recvx, fs, fr)

    for k in range(1, M):
        peer = turn(mi, k, M)
        pltpu.make_async_remote_copy(
            src_ref=pred.at[:, pl.ds(pl.multiple_of(peer * LANES, LANES), LANES)],
            dst_ref=crecv.at[mi],
            send_sem=cs,
            recv_sem=cr,
            device_id={"member": peer},
        ).start()
    own_lanes = pl.ds(pl.multiple_of(mi * LANES, LANES), LANES)
    own_chunk = pltpu.make_async_copy(pred.at[:, own_lanes], crecv.at[mi], own_sem)
    own_chunk.start()

    half = LANES // 2
    for stacked in (qst, ast):
        stacked[...] = jnp.zeros_like(stacked)

    def stack_heads(p, block, stacked):
        stacked[p, 0:nodes, 0:half] = block[:, 0:half]
        stacked[p, nodes:, half:] = block[:, half:]

    for c in range(width // 512):
        cols = slice(512 * c, 512 * c + 512)
        grads = dot(cot[0], wo[cols, :], 1, 1).astype(BF)
        for k in range(4):
            stack_heads(4 * c + k, grads[:, k * LANES : (k + 1) * LANES], ast)
    wait_bytes(qb.at[0], qr)
    wait_bytes(ww.at[0], wr)
    for p in range(pairs):
        lanes = slice(p * LANES, (p + 1) * LANES)
        inner = slice((p % 4) * LANES, (p % 4 + 1) * LANES)
        stack_heads(p, qb[p // 4, :, inner], qst)
        for stacked, weights, by_node, by_field in (
            (qst, ww[0, :, lanes], qw, qw_t),
            (ast, ww[1, :, lanes], aw, aw_t),
        ):
            by_node[p] = dot(stacked[p], weights, 1, 1).astype(BF)
            by_field[p] = dot(weights, stacked[p], 1, 1).astype(BF)

    wait_bytes(recvx.at[pl.ds(0, slots - cap)], fr)
    received = recvx[...]
    first = (lane == variables) & ((sub & (cap - 1)) == 0)
    total_area = jnp.sum(
        jnp.sum(jnp.where(first, received, 0.0), axis=0, keepdims=True), axis=1, keepdims=True
    )
    fields_t = received.T.astype(BF)

    def products(p):
        s_scr[p] = dot(qw[p], fields_t)
        g_scr[p] = dot(aw[p], fields_t)

    enc = jnp.zeros((LANES, slots), F32)
    def statistics():
        own_chunk.wait()
        wait_bytes(crecv.at[pl.ds(0, M - 1)], cr)

        own_area = area[:, own_lanes]
        part = jnp.zeros((1, LANES), F32)
        csend[:, variables // 16 * 16 :, :] = jnp.zeros((M, 16, LANES), BF)
        for row in range(0, variables, 16):
            r = slice(row, min(row + 16, variables))
            fields = [crecv[j, r, :] for j in range(M)]
            fact = truth[r, own_lanes]
            ranks = [jnp.zeros_like(fact) for _ in range(M)]
            skill = jnp.zeros_like(fact)
            for j in range(M):
                skill += jnp.abs(fields[j] - fact)
                for k in range(j + 1, M):
                    s = jnp.clip((fields[j] - fields[k]) * steep, -1.0, 1.0)
                    ranks[j] += s
                    ranks[k] -= s
            spread = sum(ranks[j] * fields[j] for j in range(M))
            crps = skill / M - (2.0 * coefficient) * spread
            part += jnp.sum(own_area * crps, axis=0, keepdims=True)
            for j in range(M):
                csend[j, r, :] = ranks[j].astype(BF)
        lsend[...] = jnp.broadcast_to(jnp.sum(part, axis=1, keepdims=True), lsend.shape)
        for k in range(1, M):
            pltpu.make_async_remote_copy(
                src_ref=lsend,
                dst_ref=lrecv.at[mi],
                send_sem=ls,
                recv_sem=lr,
                device_id={"member": turn(mi, k, M)},
            ).start()
        lrecv[mi] = lsend[...]
        for k in range(1, M):
            peer = turn(mi, k, M)
            pltpu.make_async_remote_copy(
                src_ref=csend.at[peer],
                dst_ref=cret.at[mi],
                send_sem=rs,
                recv_sem=rr,
                device_id={"member": peer},
            ).start()
        cret[mi] = csend[mi]

    products(0)
    for p in range(pairs):
        if p == 5:
            statistics()
        if p + 1 < pairs:
            products(p + 1)
        for i in range(2):
            r = slice(i * nodes, (i + 1) * nodes)
            s = s_scr[p, r, :] + bias[p, r, :]
            e = jnp.exp(s - jnp.max(s, axis=1, keepdims=True))
            g = g_scr[p, r, :]
            share = 1.0 / jnp.sum(e, axis=1, keepdims=True)
            inner = jnp.sum(e * g, axis=1, keepdims=True) * share
            w = e * share
            wts[p, r, :] = w.astype(BF)
            gs_scr[p, r, :] = (w * (g - inner)).astype(BF)
        enc += dot(qw_t[p], gs_scr[p]) + dot(aw_t[p], wts[p])

    wait_bytes(lrecv.at[pl.ds(0, M - 1)], lr)
    tile_loss = jnp.sum(lrecv[:, 0, 0:1], axis=0, keepdims=True)
    sende[...] = jnp.where(lane == variables, tile_loss, enc.T)
    send_grid(sende, recve, bs, br)

    low = iota((nodes, LANES), 1) < half
    values[...] = dot(recvx[...].astype(BF), ww[1]).astype(BF)
    for p in range(pairs):
        both = dot(wts[p], values[:, p * LANES : (p + 1) * LANES])
        att[:, p * LANES : (p + 1) * LANES] = jnp.where(low, both[:nodes], both[nodes:]).astype(BF)
    hid_o[0] = (q[...].astype(F32) + dot(att[...], wo[...])).astype(BF)

    wait_bytes(cret.at[pl.ds(0, M - 1)], rr)
    area_o[...] = total_area
    scale = (points * G) / total_area
    for chunk in range(points // LANES):
        cols = slice(chunk * LANES, (chunk + 1) * LANES)
        d = pred[:, cols] - truth[:, cols]
        s = jnp.where(d > 0, 1.0, jnp.where(d < 0, -1.0, 0.0)) / M
        slope = s - (2.0 * coefficient) * cret[chunk, 0:variables, :].astype(F32)
        base_o[:, cols] = (area[:, cols] * scale) * slope

    wait_bytes(recve.at[pl.ds(0, slots - cap)], br)
    wait_bytes(sendx.at[pl.ds(0, slots - cap)], fs)
    wait_bytes(sende.at[pl.ds(0, slots - cap)], bs)
    wait_bytes(crecv.at[pl.ds(0, M - 1)], cs)
    wait_bytes(csend.at[pl.ds(0, M - 1)], rs)
    wait_bytes(lrecv.at[pl.ds(0, M - 1)], ls)
    wait_bytes(ww.at[0], ws)
    wait_bytes(qb.at[0], qs)


def finish(cap, hid, base, recve, sel, area, hid_o, grad_o, loss_o, grad, loss, sems):
    variables, points = base.shape
    copies = [pltpu.make_async_copy(hid, hid_o, sems.at[0])]
    copies[0].start()
    back = recve[...].T
    high = back.astype(BF)
    terms = jnp.concatenate([high, (back - high.astype(F32)).astype(BF)], axis=0)
    for c in range(points // 256):
        cols = slice(256 * c, 256 * c + 256)
        both = dot(terms, sel[:, cols])
        grad[:, 0, cols] = base[:, cols] + (both[:LANES] + both[LANES:])[:variables]
        copy = pltpu.make_async_copy(grad.at[:, :, cols], grad_o.at[:, :, cols], sems.at[2 + c])
        copy.start()
        copies.append(copy)
    back = recve[...]
    first = (iota(back.shape, 1) == variables) & ((iota(back.shape, 0) & (cap - 1)) == 0)
    total = jnp.sum(jnp.where(first, back, 0.0), axis=0, keepdims=True)
    loss[...] = jnp.sum(total, axis=1, keepdims=True) / (area[...] * variables)
    copy = pltpu.make_async_copy(loss, loss_o, sems.at[1])
    copy.start()
    for c in copies + [copy]:
        c.wait()


def local(
    grid_count, member_count,
    predictions, truth, area, queries, cotangent, edge_slot, edge_count, edge_bias, send_rows,
    w_embed, w_query, w_keyval, w_out,
):
    G, M = grid_count, member_count
    variables, points = truth.shape
    nodes, width = queries.shape
    slots = send_rows.shape[1] * send_rows.shape[2]
    pairs = width // LANES
    area = area.reshape(1, points)
    edge_count = edge_count.reshape(1, nodes)
    predictions = jnp.transpose(predictions, (1, 0, 2))
    edge_slot = edge_slot.T
    send_rows = jnp.transpose(send_rows, (0, 2, 1))
    args = (
        predictions, truth, area, queries, cotangent, edge_slot, edge_count, edge_bias, send_rows,
        w_embed, w_query, w_keyval, w_out,
    )
    args = tuple(pltpu.with_memory_space_constraint(a, pltpu.HBM) for a in args)
    rank_rows = (variables + 15) // 16 * 16
    hbm_spec = pl.BlockSpec(memory_space=pltpu.HBM)
    vmem_spec = pl.BlockSpec(memory_space=pltpu.VMEM)
    vm = pltpu.VMEM
    dma = pltpu.SemaphoreType.DMA
    shapes = [a.shape for a in args]
    shapes[10] = (width, width // 2)
    shapes[11] = (width, width)
    parts = pl.pallas_call(
        functools.partial(kernel, G, M),
        out_shape=(
            vm((1, nodes, width), BF),
            vm((variables, points), F32),
            vm((slots, LANES), F32),
            vm((slots, points), BF),
            vm((1, 1), F32),
        ),
        in_specs=[hbm_spec] * len(args),
        out_specs=(vmem_spec,) * 5,
        scratch_shapes=[vm(shape, a.dtype) for shape, a in zip(shapes, args)]
        + [
            vm((variables, points), F32),
            vm((LANES, points), BF),
            vm((LANES, width), BF),
            vm((slots, LANES), F32),
            vm((slots, LANES), F32),
            vm((slots, LANES), F32),
            vm((M, variables, LANES), F32),
            vm((M, rank_rows, LANES), BF),
            vm((M, rank_rows, LANES), BF),
            vm((8, LANES), F32),
            vm((M, 8, LANES), F32),
            vm((pairs, 2 * nodes, slots), F32),
            vm((2, nodes, width // 2), BF),
            vm((pairs, 2 * nodes, LANES), BF),
            vm((pairs, 2 * nodes, LANES), BF),
            vm((2, LANES, width), BF),
            vm((pairs, 2 * nodes, LANES), BF),
            vm((pairs, LANES, 2 * nodes), BF),
            vm((pairs, 2 * nodes, LANES), BF),
            vm((pairs, LANES, 2 * nodes), BF),
            vm((slots, width), BF),
            vm((pairs, 2 * nodes, slots), F32),
            vm((pairs, 2 * nodes, slots), F32),
            vm((pairs, 2 * nodes, slots), BF),
            vm((pairs, 2 * nodes, slots), BF),
            vm((nodes, width), BF),
            dma((len(args),)),
            *([dma] * 15),
        ],
        compiler_params=pltpu.CompilerParams(
            collective_id=0, has_side_effects=True, vmem_limit_bytes=48 * 1024 * 1024
        ),
    )(*args)
    hidden, grad_pred, loss = pl.pallas_call(
        functools.partial(finish, slots // G),
        out_shape=(
            jax.ShapeDtypeStruct((1, nodes, width), BF),
            jax.ShapeDtypeStruct((variables, 1, points), F32),
            jax.ShapeDtypeStruct((1, 1), F32),
        ),
        in_specs=[vmem_spec] * 5,
        out_specs=(hbm_spec,) * 3,
        scratch_shapes=[vm((variables, 1, points), F32), vm((1, 1), F32), dma((6,))],
        compiler_params=pltpu.CompilerParams(vmem_limit_bytes=16 * 1024 * 1024),
    )(*parts)
    return hidden, jnp.transpose(grad_pred, (1, 0, 2)), loss.reshape(())


def solution(mesh):
    return jax.shard_map(
        functools.partial(local, mesh.shape["grid"], mesh.shape["member"]),
        mesh=mesh,
        in_specs=(
            P("member", None, "grid"),
            P(None, "grid"),
            P("grid"),
            P("grid", None),
            P("member", "grid", None),
            P("grid", None),
            P("grid"),
            P("grid", None),
            P("grid", None, None),
            P(),
            P(),
            P(),
            P(),
        ),
        out_specs=(P("member", "grid", None), P("member", None, "grid"), P()),
        check_vma=False,
    )
```

```python
import functools

import jax
import jax.numpy as jnp
from jax import lax
from jax.experimental import pallas as pl
from jax.experimental.pallas import tpu as pltpu
from jax.sharding import PartitionSpec as P

alpha_fair = 0.95
absent = -1e30
log2e = 1.4426950408889634
steep = 3e38

BF = jnp.bfloat16
F32 = jnp.float32
I32 = jnp.int32
LANES = 128
CHUNK = 32
GX, GZ = 4, 8


def dot(a, b, ca=1, cb=0):
    return lax.dot_general(a, b, (((ca,), (cb,)), ((), ())), preferred_element_type=F32)


def iota(shape, dim):
    return lax.broadcasted_iota(I32, shape, dim)


def lane_gather(x, idx):
    dims = lax.GatherDimensionNumbers(
        offset_dims=(),
        collapsed_slice_dims=(1,),
        start_index_map=(1,),
        operand_batching_dims=(0,),
        start_indices_batching_dims=(0,),
    )
    return lax.gather(
        x, idx[..., None], dims, (1, 1), mode=lax.GatherScatterMode.PROMISE_IN_BOUNDS
    )


def fair_coefficient(member_count):
    return alpha_fair / (2.0 * member_count * (member_count - 1)) + (1.0 - alpha_fair) / (
        2.0 * member_count * member_count
    )


def wait_bytes(ref, sem):
    pltpu.make_async_copy(ref, ref, sem).wait()


def kernel(
    grid_count,
    member_count,
    pred_h, truth_h, area_h, q_h, cot_h, es_h, ec_h, eb_h, sr_h, we_h, wq_h, wkv_h, wo_h,
    hid_o, base_o, recve, sel, area_o,
    predl, truth, area, q, cot, es_t, ec, eb, sr, we, wq, wkv, wo,
    pred, predp, wep, sendx, recvx, sende, crecv, csend, cret, lsend, lrecv,
    bias, qb, qst, ast, ww, qw, qw_t, aw, aw_t, values, s_scr, g_scr, gs_scr, wts, att,
    ld_sem, own_sem, fs, fr, cs, cr, rs, rr, ls, lr, bs, br, ws, wr, qs, qr,
):
    G, M = grid_count, member_count
    gi = lax.axis_index("grid")
    mi = lax.axis_index("member")
    variables, points = pred.shape
    nodes, width = q.shape
    pairs = width // LANES
    slots = sendx.shape[0]
    cap = slots // G
    fan = es_t.shape[0]
    coefficient = fair_coefficient(M)

    core = lax.rem(mi, 2)
    partner = mi + 1 - 2 * core
    wq_h = wq_h.at[:, pl.ds(pl.multiple_of(core * (width // 2), LANES), width // 2)]
    wkv_h = wkv_h.at[:, pl.ds(pl.multiple_of(core * width, LANES), width)]
    sources = [sr_h, pred_h, area_h, we_h, wkv_h, q_h, wq_h, es_h, ec_h, eb_h, cot_h, wo_h, truth_h]
    targets = [sr, predl, area, we, wkv, q, wq, es_t, ec, eb, cot, wo, truth]
    loads = [
        pltpu.make_async_copy(s, t, ld_sem.at[i]) for i, (s, t) in enumerate(zip(sources, targets))
    ]
    for c in loads[:4]:
        c.start()

    barrier = pltpu.get_barrier_semaphore()

    def turn(index, k, count):
        moved = index + k
        return jnp.where(moved >= count, moved - count, moved)

    gx, gz = lax.div(gi, GZ), lax.rem(gi, GZ)
    steps = [(dx, dz) for dx in range(GX) for dz in range(GZ)][1:]
    steps.sort(key=lambda d: -(min(d[0], GX - d[0]) + min(d[1], GZ - d[1])))
    tiles = [turn(gx, dx, GX) * GZ + turn(gz, dz, GZ) for dx, dz in steps]
    for peer in tiles:
        pl.semaphore_signal(barrier, inc=1, device_id={"grid": peer})
    for k in range(1, M):
        pl.semaphore_signal(barrier, inc=1, device_id={"member": turn(mi, k, M)})
    for c in loads[4:]:
        c.start()

    loads[0].wait()
    spots = jnp.broadcast_to(sr[0].astype(F32)[None], (G, cap, G)).reshape(slots, G)
    pick = iota((slots, G), 1) == (iota((slots, G), 0) // cap)
    rows = jnp.sum(jnp.where(pick, spots, 0.0), axis=1, keepdims=True).astype(I32)
    for c in range(slots // 64):
        r = pl.ds(64 * c, 64)
        hit = iota((64, points), 1) == rows[64 * c : 64 * c + 64]
        sel[r, :] = jnp.where(hit, 1.0, 0.0).astype(BF)
    predp[...] = jnp.zeros_like(predp)
    wep[...] = jnp.zeros_like(wep)
    for c in loads[1:4]:
        c.wait()
    pred[...] = predl[:, 0, :]
    predp[0:variables, :] = pred[...].astype(BF)
    tile_area = jnp.sum(area[...], axis=1, keepdims=True)
    lane = iota((slots, LANES), 1)
    sub = iota((slots, LANES), 0)
    x = dot(sel[...], predp[...], 1, 1)
    sendx[...] = jnp.where(lane == variables, tile_area, x)


    for c in loads[4:7]:
        c.wait()
    wep[0:variables, :] = we[...]
    for c in range(width // 512):
        cols = slice(512 * c, 512 * c + 512)
        ww[core, :, cols] = dot(wep[...], wkv[:, cols]).astype(BF)
    qb[core] = (dot(q[...], wq[...]) * 0.125).astype(BF)

    for c in loads[7:]:
        c.wait()
    pl.semaphore_wait(barrier, G - 1 + M - 1)

    def hand_over(ref, s_sem, r_sem):
        return pltpu.make_async_remote_copy(
            src_ref=ref.at[core],
            dst_ref=ref.at[core],
            send_sem=s_sem,
            recv_sem=r_sem,
            device_id={"member": partner},
        )

    hand_over(ww, ws, wr).start()
    hand_over(qb, qs, qr).start()

    mine = pl.ds(pl.multiple_of(gi * cap, cap), cap)

    def send_grid(src, dst, s_sem, r_sem):
        for peer in tiles:
            theirs = pl.ds(pl.multiple_of(peer * cap, cap), cap)
            pltpu.make_async_remote_copy(
                src_ref=src.at[theirs],
                dst_ref=dst.at[mine],
                send_sem=s_sem,
                recv_sem=r_sem,
                device_id={"grid": peer},
            ).start()
        dst[mine, :] = src[mine, :]

    send_grid(sendx, recvx, fs, fr)

    for k in range(1, M):
        peer = turn(mi, k, M)
        pltpu.make_async_remote_copy(
            src_ref=pred.at[:, pl.ds(pl.multiple_of(peer * LANES, LANES), LANES)],
            dst_ref=crecv.at[mi],
            send_sem=cs,
            recv_sem=cr,
            device_id={"member": peer},
        ).start()
    own_lanes = pl.ds(pl.multiple_of(mi * LANES, LANES), LANES)
    own_chunk = pltpu.make_async_copy(pred.at[:, own_lanes], crecv.at[mi], own_sem)
    own_chunk.start()

    real = iota((fan, nodes), 0) < ec[...]
    es = jnp.where(real, es_t[...], -1).astype(F32).T.astype(I32)

    def spread_bias(start):
        r = slice(start, start + CHUNK)
        edges = es[r, :]
        slot_ids = iota((CHUNK, slots), 1)
        inverse = jnp.full((CHUNK, slots), -1, I32)
        for e in range(fan):
            inverse = jnp.where(edges[:, e : e + 1] == slot_ids, e, inverse)
        there = inverse >= 0
        index = jnp.maximum(inverse, 0)
        columns = [eb[r, j * LANES : (j + 1) * LANES] * log2e for j in range(4)]
        l = iota((CHUNK, LANES), 1)
        edge = l & (fan - 1)
        for t in range(4):
            place = (edge & 7) * 16 + 4 * t + (l >> 5)
            table = lane_gather(columns[0], place)
            for j in range(1, 4):
                table = jnp.where((edge >> 3) == j, lane_gather(columns[j], place), table)
            for hh in range(4):
                h = 4 * t + hh
                rows_of = slice((h % 2) * nodes + start, (h % 2) * nodes + start + CHUNK)
                for side in range(slots // LANES):
                    cols = slice(side * LANES, (side + 1) * LANES)
                    got = lane_gather(table, index[:, cols] + 32 * hh)
                    bias[h // 2, rows_of, cols] = jnp.where(
                        there[:, cols], got, absent
                    )

    half = LANES // 2
    for stacked in (qst, ast):
        stacked[...] = jnp.zeros_like(stacked)

    def stack_heads(p, block, stacked):
        stacked[p, 0:nodes, 0:half] = block[:, 0:half]
        stacked[p, nodes:, half:] = block[:, half:]

    for c in range(width // 512):
        cols = slice(512 * c, 512 * c + 512)
        grads = dot(cot[0], wo[cols, :], 1, 1).astype(BF)
        spread_bias(2 * c * CHUNK)
        spread_bias((2 * c + 1) * CHUNK)
        for k in range(4):
            stack_heads(4 * c + k, grads[:, k * LANES : (k + 1) * LANES], ast)
    wait_bytes(qb.at[0], qr)
    wait_bytes(ww.at[0], wr)
    for p in range(pairs):
        lanes = slice(p * LANES, (p + 1) * LANES)
        inner = slice((p % 4) * LANES, (p % 4 + 1) * LANES)
        stack_heads(p, qb[p // 4, :, inner], qst)
        for stacked, weights, by_node, by_field, factor in (
            (qst, ww[0, :, lanes], qw, qw_t, log2e),
            (ast, ww[1, :, lanes], aw, aw_t, 1.0),
        ):
            by_node[p] = (dot(stacked[p], weights, 1, 1) * factor).astype(BF)
            by_field[p] = dot(weights, stacked[p], 1, 1).astype(BF)

    wait_bytes(recvx.at[pl.ds(0, slots - cap)], fr)
    received = recvx[...]
    first = (lane == variables) & ((sub & (cap - 1)) == 0)
    total_area = jnp.sum(
        jnp.sum(jnp.where(first, received, 0.0), axis=0, keepdims=True), axis=1, keepdims=True
    )
    fields_t = received.T.astype(BF)

    def products(p):
        s_scr[p] = dot(qw[p], fields_t)
        g_scr[p] = dot(aw[p], fields_t)

    enc = jnp.zeros((LANES, slots), F32)
    def statistics():
        own_chunk.wait()
        wait_bytes(crecv.at[pl.ds(0, M - 1)], cr)

        own_area = area[:, own_lanes]
        part = jnp.zeros((1, LANES), F32)
        csend[:, variables // 16 * 16 :, :] = jnp.zeros((M, 16, LANES), BF)
        for row in range(0, variables, 16):
            r = slice(row, min(row + 16, variables))
            fields = [crecv[j, r, :] for j in range(M)]
            fact = truth[r, own_lanes]
            ranks = [jnp.zeros_like(fact) for _ in range(M)]
            skill = jnp.zeros_like(fact)
            for j in range(M):
                skill += jnp.abs(fields[j] - fact)
                for k in range(j + 1, M):
                    s = jnp.clip((fields[j] - fields[k]) * steep, -1.0, 1.0)
                    ranks[j] += s
                    ranks[k] -= s
            spread = sum(ranks[j] * fields[j] for j in range(M))
            crps = skill / M - (2.0 * coefficient) * spread
            part += jnp.sum(own_area * crps, axis=0, keepdims=True)
            for j in range(M):
                csend[j, r, :] = ranks[j].astype(BF)
        lsend[...] = jnp.broadcast_to(jnp.sum(part, axis=1, keepdims=True), lsend.shape)
        for k in range(1, M):
            pltpu.make_async_remote_copy(
                src_ref=lsend,
                dst_ref=lrecv.at[mi],
                send_sem=ls,
                recv_sem=lr,
                device_id={"member": turn(mi, k, M)},
            ).start()
        lrecv[mi] = lsend[...]
        for k in range(1, M):
            peer = turn(mi, k, M)
            pltpu.make_async_remote_copy(
                src_ref=csend.at[peer],
                dst_ref=cret.at[mi],
                send_sem=rs,
                recv_sem=rr,
                device_id={"member": peer},
            ).start()
        cret[mi] = csend[mi]

    products(0)
    for p in range(pairs):
        if p == 5:
            statistics()
        if p + 1 < pairs:
            products(p + 1)
        for i in range(2 * nodes // 64):
            r = slice(i * 64, (i + 1) * 64)
            s = s_scr[p, r, :] + bias[p, r, :]
            e = jnp.exp2(s - jnp.max(s, axis=1, keepdims=True))
            g = g_scr[p, r, :]
            share = 1.0 / jnp.sum(e, axis=1, keepdims=True)
            inner = jnp.sum(e * g, axis=1, keepdims=True) * share
            w = e * share
            wts[p, r, :] = w.astype(BF)
            gs_scr[p, r, :] = (w * (g - inner)).astype(BF)
        enc += dot(qw_t[p], gs_scr[p]) + dot(aw_t[p], wts[p])

    wait_bytes(lrecv.at[pl.ds(0, M - 1)], lr)
    tile_loss = jnp.sum(lrecv[:, 0, 0:1], axis=0, keepdims=True)
    sende[...] = jnp.where(lane == variables, tile_loss, enc.T)
    send_grid(sende, recve, bs, br)

    low = iota((nodes, LANES), 1) < half
    values[...] = dot(recvx[...].astype(BF), ww[1]).astype(BF)
    for p in range(pairs):
        both = dot(wts[p], values[:, p * LANES : (p + 1) * LANES])
        att[:, p * LANES : (p + 1) * LANES] = jnp.where(low, both[:nodes], both[nodes:]).astype(BF)
    hid_o[0] = (q[...].astype(F32) + dot(att[...], wo[...])).astype(BF)

    wait_bytes(cret.at[pl.ds(0, M - 1)], rr)
    area_o[...] = total_area
    scale = (points * G) / total_area
    for chunk in range(points // LANES):
        cols = slice(chunk * LANES, (chunk + 1) * LANES)
        d = pred[:, cols] - truth[:, cols]
        s = jnp.where(d > 0, 1.0, jnp.where(d < 0, -1.0, 0.0)) / M
        slope = s - (2.0 * coefficient) * cret[chunk, 0:variables, :].astype(F32)
        base_o[:, cols] = (area[:, cols] * scale) * slope

    wait_bytes(recve.at[pl.ds(0, slots - cap)], br)
    wait_bytes(sendx.at[pl.ds(0, slots - cap)], fs)
    wait_bytes(sende.at[pl.ds(0, slots - cap)], bs)
    wait_bytes(crecv.at[pl.ds(0, M - 1)], cs)
    wait_bytes(csend.at[pl.ds(0, M - 1)], rs)
    wait_bytes(lrecv.at[pl.ds(0, M - 1)], ls)
    wait_bytes(ww.at[0], ws)
    wait_bytes(qb.at[0], qs)


def finish(cap, hid, base, recve, sel, area, hid_o, grad_o, loss_o, grad, loss, sems):
    variables, points = base.shape
    copies = [pltpu.make_async_copy(hid, hid_o, sems.at[0])]
    copies[0].start()
    back = recve[...].T
    high = back.astype(BF)
    terms = jnp.concatenate([high, (back - high.astype(F32)).astype(BF)], axis=0)
    for c in range(points // 512):
        cols = slice(512 * c, 512 * c + 512)
        both = dot(terms, sel[:, cols])
        grad[:, 0, cols] = base[:, cols] + (both[:LANES] + both[LANES:])[:variables]
        copy = pltpu.make_async_copy(grad.at[:, :, cols], grad_o.at[:, :, cols], sems.at[2 + c])
        copy.start()
        copies.append(copy)
    back = recve[...]
    first = (iota(back.shape, 1) == variables) & ((iota(back.shape, 0) & (cap - 1)) == 0)
    total = jnp.sum(jnp.where(first, back, 0.0), axis=0, keepdims=True)
    loss[...] = jnp.sum(total, axis=1, keepdims=True) / (area[...] * variables)
    copy = pltpu.make_async_copy(loss, loss_o, sems.at[1])
    copy.start()
    for c in copies + [copy]:
        c.wait()


def local(
    grid_count, member_count,
    predictions, truth, area, queries, cotangent, edge_slot, edge_count, edge_bias, send_rows,
    w_embed, w_query, w_keyval, w_out,
):
    G, M = grid_count, member_count
    variables, points = truth.shape
    nodes, width = queries.shape
    slots = send_rows.shape[1] * send_rows.shape[2]
    pairs = width // LANES
    area = area.reshape(1, points)
    edge_count = edge_count.reshape(1, nodes)
    predictions = jnp.transpose(predictions, (1, 0, 2))
    edge_slot = edge_slot.T
    send_rows = jnp.transpose(send_rows, (0, 2, 1))
    args = (
        predictions, truth, area, queries, cotangent, edge_slot, edge_count, edge_bias, send_rows,
        w_embed, w_query, w_keyval, w_out,
    )
    args = tuple(pltpu.with_memory_space_constraint(a, pltpu.HBM) for a in args)
    rank_rows = (variables + 15) // 16 * 16
    hbm_spec = pl.BlockSpec(memory_space=pltpu.HBM)
    vmem_spec = pl.BlockSpec(memory_space=pltpu.VMEM)
    vm = pltpu.VMEM
    dma = pltpu.SemaphoreType.DMA
    shapes = [a.shape for a in args]
    shapes[10] = (width, width // 2)
    shapes[11] = (width, width)
    parts = pl.pallas_call(
        functools.partial(kernel, G, M),
        out_shape=(
            vm((1, nodes, width), BF),
            vm((variables, points), F32),
            vm((slots, LANES), F32),
            vm((slots, points), BF),
            vm((1, 1), F32),
        ),
        in_specs=[hbm_spec] * len(args),
        out_specs=(vmem_spec,) * 5,
        scratch_shapes=[vm(shape, a.dtype) for shape, a in zip(shapes, args)]
        + [
            vm((variables, points), F32),
            vm((LANES, points), BF),
            vm((LANES, width), BF),
            vm((slots, LANES), F32),
            vm((slots, LANES), F32),
            vm((slots, LANES), F32),
            vm((M, variables, LANES), F32),
            vm((M, rank_rows, LANES), BF),
            vm((M, rank_rows, LANES), BF),
            vm((8, LANES), F32),
            vm((M, 8, LANES), F32),
            vm((pairs, 2 * nodes, slots), F32),
            vm((2, nodes, width // 2), BF),
            vm((pairs, 2 * nodes, LANES), BF),
            vm((pairs, 2 * nodes, LANES), BF),
            vm((2, LANES, width), BF),
            vm((pairs, 2 * nodes, LANES), BF),
            vm((pairs, LANES, 2 * nodes), BF),
            vm((pairs, 2 * nodes, LANES), BF),
            vm((pairs, LANES, 2 * nodes), BF),
            vm((slots, width), BF),
            vm((pairs, 2 * nodes, slots), F32),
            vm((pairs, 2 * nodes, slots), F32),
            vm((pairs, 2 * nodes, slots), BF),
            vm((pairs, 2 * nodes, slots), BF),
            vm((nodes, width), BF),
            dma((len(args),)),
            *([dma] * 15),
        ],
        compiler_params=pltpu.CompilerParams(
            collective_id=0, has_side_effects=True, vmem_limit_bytes=48 * 1024 * 1024
        ),
    )(*args)
    hidden, grad_pred, loss = pl.pallas_call(
        functools.partial(finish, slots // G),
        out_shape=(
            jax.ShapeDtypeStruct((1, nodes, width), BF),
            jax.ShapeDtypeStruct((variables, 1, points), F32),
            jax.ShapeDtypeStruct((1, 1), F32),
        ),
        in_specs=[vmem_spec] * 5,
        out_specs=(hbm_spec,) * 3,
        scratch_shapes=[vm((variables, 1, points), F32), vm((1, 1), F32), dma((4,))],
        compiler_params=pltpu.CompilerParams(vmem_limit_bytes=16 * 1024 * 1024),
    )(*parts)
    return hidden, jnp.transpose(grad_pred, (1, 0, 2)), loss.reshape(())


def solution(mesh):
    return jax.shard_map(
        functools.partial(local, mesh.shape["grid"], mesh.shape["member"]),
        mesh=mesh,
        in_specs=(
            P("member", None, "grid"),
            P(None, "grid"),
            P("grid"),
            P("grid", None),
            P("member", "grid", None),
            P("grid", None),
            P("grid"),
            P("grid", None),
            P("grid", None, None),
            P(),
            P(),
            P(),
            P(),
        ),
        out_specs=(P("member", "grid", None), P("member", None, "grid"), P()),
        check_vma=False,
    )
```

```python
import functools

import jax
import jax.numpy as jnp
from jax import lax
from jax.experimental import pallas as pl
from jax.experimental.pallas import tpu as pltpu
from jax.sharding import PartitionSpec as P

alpha_fair = 0.95
absent = -1e30
log2e = 1.4426950408889634
steep = 3e38

BF = jnp.bfloat16
F32 = jnp.float32
I32 = jnp.int32
LANES = 128
CHUNK = 32
GX, GZ = 4, 8


def dot(a, b, ca=1, cb=0):
    return lax.dot_general(a, b, (((ca,), (cb,)), ((), ())), preferred_element_type=F32)


def iota(shape, dim):
    return lax.broadcasted_iota(I32, shape, dim)


def lane_gather(x, idx):
    dims = lax.GatherDimensionNumbers(
        offset_dims=(),
        collapsed_slice_dims=(1,),
        start_index_map=(1,),
        operand_batching_dims=(0,),
        start_indices_batching_dims=(0,),
    )
    return lax.gather(
        x, idx[..., None], dims, (1, 1), mode=lax.GatherScatterMode.PROMISE_IN_BOUNDS
    )


def fair_coefficient(member_count):
    return alpha_fair / (2.0 * member_count * (member_count - 1)) + (1.0 - alpha_fair) / (
        2.0 * member_count * member_count
    )


def wait_bytes(ref, sem):
    pltpu.make_async_copy(ref, ref, sem).wait()


def kernel(
    grid_count,
    member_count,
    pred_h, truth_h, area_h, q_h, cot_h, es_h, ec_h, eb_h, sr_h, we_h, wq_h, wkv_h, wo_h,
    hid_o, base_o, recve, sel, area_o,
    predl, truth, area, q, cot, es_t, ec, eb, sr, we, wq, wkv, wo,
    pred, predp, wep, sendx, recvx, sende, crecv, csend, cret, lsend, lrecv,
    bias, qb, qst, ast, ww, qw, qw_t, aw, aw_t, values, s_scr, g_scr, gs_scr, wts, att,
    ld_sem, own_sem, fs, fr, cs, cr, rs, rr, ls, lr, bs, br, ws, wr, qs, qr,
):
    G, M = grid_count, member_count
    gi = lax.axis_index("grid")
    mi = lax.axis_index("member")
    variables, points = pred.shape
    nodes, width = q.shape
    pairs = width // LANES
    slots = sendx.shape[0]
    cap = slots // G
    fan = es_t.shape[0]
    coefficient = fair_coefficient(M)

    core = lax.rem(mi, 2)
    partner = mi + 1 - 2 * core
    wq_h = wq_h.at[:, pl.ds(pl.multiple_of(core * (width // 2), LANES), width // 2)]
    wkv_h = wkv_h.at[:, pl.ds(pl.multiple_of(core * width, LANES), width)]
    sources = [sr_h, pred_h, area_h, we_h, wkv_h, q_h, wq_h, es_h, ec_h, eb_h, cot_h, wo_h, truth_h]
    targets = [sr, predl, area, we, wkv, q, wq, es_t, ec, eb, cot, wo, truth]
    loads = [
        pltpu.make_async_copy(s, t, ld_sem.at[i]) for i, (s, t) in enumerate(zip(sources, targets))
    ]
    for c in loads[:4]:
        c.start()

    barrier = pltpu.get_barrier_semaphore()

    def turn(index, k, count):
        moved = index + k
        return jnp.where(moved >= count, moved - count, moved)

    gx, gz = lax.div(gi, GZ), lax.rem(gi, GZ)
    steps = [(dx, dz) for dx in range(GX) for dz in range(GZ)][1:]
    steps.sort(key=lambda d: -(min(d[0], GX - d[0]) + min(d[1], GZ - d[1])))
    tiles = [turn(gx, dx, GX) * GZ + turn(gz, dz, GZ) for dx, dz in steps]
    for peer in tiles:
        pl.semaphore_signal(barrier, inc=1, device_id={"grid": peer})
    for k in range(1, M):
        pl.semaphore_signal(barrier, inc=1, device_id={"member": turn(mi, k, M)})
    for c in loads[4:]:
        c.start()

    loads[0].wait()
    spots = jnp.broadcast_to(sr[0].astype(F32)[None], (G, cap, G)).reshape(slots, G)
    pick = iota((slots, G), 1) == (iota((slots, G), 0) // cap)
    rows = jnp.sum(jnp.where(pick, spots, 0.0), axis=1, keepdims=True).astype(I32)
    for c in range(slots // 64):
        r = pl.ds(64 * c, 64)
        hit = iota((64, points), 1) == rows[64 * c : 64 * c + 64]
        sel[r, :] = jnp.where(hit, 1.0, 0.0).astype(BF)
    predp[...] = jnp.zeros_like(predp)
    wep[...] = jnp.zeros_like(wep)
    for c in loads[1:4]:
        c.wait()
    pred[...] = predl[:, 0, :]
    predp[0:variables, :] = pred[...].astype(BF)
    tile_area = jnp.sum(area[...], axis=1, keepdims=True)
    lane = iota((slots, LANES), 1)
    sub = iota((slots, LANES), 0)
    x = dot(sel[...], predp[...], 1, 1)
    sendx[...] = jnp.where(lane == variables, tile_area, x)


    for c in loads[4:]:
        c.wait()
    real = iota((fan, nodes), 0) < ec[...]
    es = jnp.where(real, es_t[...], -1).astype(F32).T.astype(I32)

    def spread_bias(start):
        r = slice(start, start + CHUNK)
        edges = es[r, :]
        slot_ids = iota((CHUNK, slots), 1)
        inverse = jnp.full((CHUNK, slots), -1, I32)
        for e in range(fan):
            inverse = jnp.where(edges[:, e : e + 1] == slot_ids, e, inverse)
        there = inverse >= 0
        index = jnp.maximum(inverse, 0)
        columns = [eb[r, j * LANES : (j + 1) * LANES] * log2e for j in range(4)]
        l = iota((CHUNK, LANES), 1)
        edge = l & (fan - 1)
        for t in range(4):
            place = (edge & 7) * 16 + 4 * t + (l >> 5)
            table = lane_gather(columns[0], place)
            for j in range(1, 4):
                table = jnp.where((edge >> 3) == j, lane_gather(columns[j], place), table)
            for hh in range(4):
                h = 4 * t + hh
                rows_of = slice((h % 2) * nodes + start, (h % 2) * nodes + start + CHUNK)
                for side in range(slots // LANES):
                    cols = slice(side * LANES, (side + 1) * LANES)
                    got = lane_gather(table, index[:, cols] + 32 * hh)
                    bias[h // 2, rows_of, cols] = jnp.where(
                        there[:, cols], got, absent
                    )

    for c in range(2):
        spread_bias(c * CHUNK)

    pl.semaphore_wait(barrier, G - 1 + M - 1)
    for k in range(1, M):
        peer = turn(mi, k, M)
        pltpu.make_async_remote_copy(
            src_ref=pred.at[:, pl.ds(pl.multiple_of(peer * LANES, LANES), LANES)],
            dst_ref=crecv.at[mi],
            send_sem=cs,
            recv_sem=cr,
            device_id={"member": peer},
        ).start()
    own_lanes = pl.ds(pl.multiple_of(mi * LANES, LANES), LANES)
    own_chunk = pltpu.make_async_copy(pred.at[:, own_lanes], crecv.at[mi], own_sem)
    own_chunk.start()

    mine = pl.ds(pl.multiple_of(gi * cap, cap), cap)

    def send_grid(src, dst, s_sem, r_sem):
        for peer in tiles:
            theirs = pl.ds(pl.multiple_of(peer * cap, cap), cap)
            pltpu.make_async_remote_copy(
                src_ref=src.at[theirs],
                dst_ref=dst.at[mine],
                send_sem=s_sem,
                recv_sem=r_sem,
                device_id={"grid": peer},
            ).start()
        dst[mine, :] = src[mine, :]

    send_grid(sendx, recvx, fs, fr)

    wep[0:variables, :] = we[...]
    for c in range(width // 512):
        cols = slice(512 * c, 512 * c + 512)
        ww[core, :, cols] = dot(wep[...], wkv[:, cols]).astype(BF)
    qb[core] = (dot(q[...], wq[...]) * 0.125).astype(BF)

    def hand_over(ref, s_sem, r_sem):
        return pltpu.make_async_remote_copy(
            src_ref=ref.at[core],
            dst_ref=ref.at[core],
            send_sem=s_sem,
            recv_sem=r_sem,
            device_id={"member": partner},
        )

    hand_over(ww, ws, wr).start()
    hand_over(qb, qs, qr).start()


    half = LANES // 2
    for stacked in (qst, ast):
        stacked[...] = jnp.zeros_like(stacked)

    def stack_heads(p, block, stacked):
        stacked[p, 0:nodes, 0:half] = block[:, 0:half]
        stacked[p, nodes:, half:] = block[:, half:]

    for c in range(width // 512):
        cols = slice(512 * c, 512 * c + 512)
        grads = dot(cot[0], wo[cols, :], 1, 1).astype(BF)
        spread_bias((2 + c) * CHUNK)
        for k in range(4):
            stack_heads(4 * c + k, grads[:, k * LANES : (k + 1) * LANES], ast)
    wait_bytes(qb.at[0], qr)
    wait_bytes(ww.at[0], wr)
    for p in range(pairs):
        lanes = slice(p * LANES, (p + 1) * LANES)
        inner = slice((p % 4) * LANES, (p % 4 + 1) * LANES)
        stack_heads(p, qb[p // 4, :, inner], qst)
        for stacked, weights, by_node, by_field, factor in (
            (qst, ww[0, :, lanes], qw, qw_t, log2e),
            (ast, ww[1, :, lanes], aw, aw_t, 1.0),
        ):
            by_node[p] = (dot(stacked[p], weights, 1, 1) * factor).astype(BF)
            by_field[p] = dot(weights, stacked[p], 1, 1).astype(BF)

    wait_bytes(recvx.at[pl.ds(0, slots - cap)], fr)
    received = recvx[...]
    first = (lane == variables) & ((sub & (cap - 1)) == 0)
    total_area = jnp.sum(
        jnp.sum(jnp.where(first, received, 0.0), axis=0, keepdims=True), axis=1, keepdims=True
    )
    fields_t = received.T.astype(BF)

    def products(p):
        s_scr[p] = dot(qw[p], fields_t)
        g_scr[p] = dot(aw[p], fields_t)

    enc = jnp.zeros((LANES, slots), F32)
    def statistics():
        own_chunk.wait()
        wait_bytes(crecv.at[pl.ds(0, M - 1)], cr)

        own_area = area[:, own_lanes]
        part = jnp.zeros((1, LANES), F32)
        csend[:, variables // 16 * 16 :, :] = jnp.zeros((M, 16, LANES), BF)
        for row in range(0, variables, 16):
            r = slice(row, min(row + 16, variables))
            fields = [crecv[j, r, :] for j in range(M)]
            fact = truth[r, own_lanes]
            ranks = [jnp.zeros_like(fact) for _ in range(M)]
            skill = jnp.zeros_like(fact)
            for j in range(M):
                skill += jnp.abs(fields[j] - fact)
                for k in range(j + 1, M):
                    s = jnp.clip((fields[j] - fields[k]) * steep, -1.0, 1.0)
                    ranks[j] += s
                    ranks[k] -= s
            spread = sum(ranks[j] * fields[j] for j in range(M))
            crps = skill / M - (2.0 * coefficient) * spread
            part += jnp.sum(own_area * crps, axis=0, keepdims=True)
            for j in range(M):
                csend[j, r, :] = ranks[j].astype(BF)
        lsend[...] = jnp.broadcast_to(jnp.sum(part, axis=1, keepdims=True), lsend.shape)
        for k in range(1, M):
            pltpu.make_async_remote_copy(
                src_ref=lsend,
                dst_ref=lrecv.at[mi],
                send_sem=ls,
                recv_sem=lr,
                device_id={"member": turn(mi, k, M)},
            ).start()
        lrecv[mi] = lsend[...]
        for k in range(1, M):
            peer = turn(mi, k, M)
            pltpu.make_async_remote_copy(
                src_ref=csend.at[peer],
                dst_ref=cret.at[mi],
                send_sem=rs,
                recv_sem=rr,
                device_id={"member": peer},
            ).start()
        cret[mi] = csend[mi]

    products(0)
    for p in range(pairs):
        if p == 3:
            statistics()
        if p + 1 < pairs:
            products(p + 1)
        for i in range(2 * nodes // 64):
            r = slice(i * 64, (i + 1) * 64)
            s = s_scr[p, r, :] + bias[p, r, :]
            e = jnp.exp2(s - jnp.max(s, axis=1, keepdims=True))
            g = g_scr[p, r, :]
            share = 1.0 / jnp.sum(e, axis=1, keepdims=True)
            inner = jnp.sum(e * g, axis=1, keepdims=True) * share
            w = e * share
            wts[p, r, :] = w.astype(BF)
            gs_scr[p, r, :] = (w * (g - inner)).astype(BF)
        enc += dot(qw_t[p], gs_scr[p]) + dot(aw_t[p], wts[p])

    wait_bytes(lrecv.at[pl.ds(0, M - 1)], lr)
    tile_loss = jnp.sum(lrecv[:, 0, 0:1], axis=0, keepdims=True)
    sende[...] = jnp.where(lane == variables, tile_loss, enc.T)
    send_grid(sende, recve, bs, br)

    low = iota((nodes, LANES), 1) < half
    values[...] = dot(recvx[...].astype(BF), ww[1]).astype(BF)
    for p in range(pairs):
        both = dot(wts[p], values[:, p * LANES : (p + 1) * LANES])
        att[:, p * LANES : (p + 1) * LANES] = jnp.where(low, both[:nodes], both[nodes:]).astype(BF)
    hid_o[0] = (q[...].astype(F32) + dot(att[...], wo[...])).astype(BF)

    wait_bytes(cret.at[pl.ds(0, M - 1)], rr)
    area_o[...] = total_area
    scale = (points * G) / total_area
    for chunk in range(points // LANES):
        cols = slice(chunk * LANES, (chunk + 1) * LANES)
        d = pred[:, cols] - truth[:, cols]
        s = jnp.where(d > 0, 1.0, jnp.where(d < 0, -1.0, 0.0)) / M
        slope = s - (2.0 * coefficient) * cret[chunk, 0:variables, :].astype(F32)
        base_o[:, cols] = (area[:, cols] * scale) * slope

    wait_bytes(recve.at[pl.ds(0, slots - cap)], br)
    wait_bytes(sendx.at[pl.ds(0, slots - cap)], fs)
    wait_bytes(sende.at[pl.ds(0, slots - cap)], bs)
    wait_bytes(crecv.at[pl.ds(0, M - 1)], cs)
    wait_bytes(csend.at[pl.ds(0, M - 1)], rs)
    wait_bytes(lrecv.at[pl.ds(0, M - 1)], ls)
    wait_bytes(ww.at[0], ws)
    wait_bytes(qb.at[0], qs)


def finish(cap, hid, base, recve, sel, area, hid_o, grad_o, loss_o, grad, loss, sems):
    variables, points = base.shape
    copies = [pltpu.make_async_copy(hid, hid_o, sems.at[0])]
    copies[0].start()
    back = recve[...].T
    high = back.astype(BF)
    terms = jnp.concatenate([high, (back - high.astype(F32)).astype(BF)], axis=0)
    for c in range(points // 512):
        cols = slice(512 * c, 512 * c + 512)
        both = dot(terms, sel[:, cols])
        grad[:, 0, cols] = base[:, cols] + (both[:LANES] + both[LANES:])[:variables]
        copy = pltpu.make_async_copy(grad.at[:, :, cols], grad_o.at[:, :, cols], sems.at[2 + c])
        copy.start()
        copies.append(copy)
    back = recve[...]
    first = (iota(back.shape, 1) == variables) & ((iota(back.shape, 0) & (cap - 1)) == 0)
    total = jnp.sum(jnp.where(first, back, 0.0), axis=0, keepdims=True)
    loss[...] = jnp.sum(total, axis=1, keepdims=True) / (area[...] * variables)
    copy = pltpu.make_async_copy(loss, loss_o, sems.at[1])
    copy.start()
    for c in copies + [copy]:
        c.wait()


def local(
    grid_count, member_count,
    predictions, truth, area, queries, cotangent, edge_slot, edge_count, edge_bias, send_rows,
    w_embed, w_query, w_keyval, w_out,
):
    G, M = grid_count, member_count
    variables, points = truth.shape
    nodes, width = queries.shape
    slots = send_rows.shape[1] * send_rows.shape[2]
    pairs = width // LANES
    area = area.reshape(1, points)
    edge_count = edge_count.reshape(1, nodes)
    predictions = jnp.transpose(predictions, (1, 0, 2))
    edge_slot = edge_slot.T
    send_rows = jnp.transpose(send_rows, (0, 2, 1))
    args = (
        predictions, truth, area, queries, cotangent, edge_slot, edge_count, edge_bias, send_rows,
        w_embed, w_query, w_keyval, w_out,
    )
    args = tuple(pltpu.with_memory_space_constraint(a, pltpu.HBM) for a in args)
    rank_rows = (variables + 15) // 16 * 16
    hbm_spec = pl.BlockSpec(memory_space=pltpu.HBM)
    vmem_spec = pl.BlockSpec(memory_space=pltpu.VMEM)
    vm = pltpu.VMEM
    dma = pltpu.SemaphoreType.DMA
    shapes = [a.shape for a in args]
    shapes[10] = (width, width // 2)
    shapes[11] = (width, width)
    parts = pl.pallas_call(
        functools.partial(kernel, G, M),
        out_shape=(
            vm((1, nodes, width), BF),
            vm((variables, points), F32),
            vm((slots, LANES), F32),
            vm((slots, points), BF),
            vm((1, 1), F32),
        ),
        in_specs=[hbm_spec] * len(args),
        out_specs=(vmem_spec,) * 5,
        scratch_shapes=[vm(shape, a.dtype) for shape, a in zip(shapes, args)]
        + [
            vm((variables, points), F32),
            vm((LANES, points), BF),
            vm((LANES, width), BF),
            vm((slots, LANES), F32),
            vm((slots, LANES), F32),
            vm((slots, LANES), F32),
            vm((M, variables, LANES), F32),
            vm((M, rank_rows, LANES), BF),
            vm((M, rank_rows, LANES), BF),
            vm((8, LANES), F32),
            vm((M, 8, LANES), F32),
            vm((pairs, 2 * nodes, slots), F32),
            vm((2, nodes, width // 2), BF),
            vm((pairs, 2 * nodes, LANES), BF),
            vm((pairs, 2 * nodes, LANES), BF),
            vm((2, LANES, width), BF),
            vm((pairs, 2 * nodes, LANES), BF),
            vm((pairs, LANES, 2 * nodes), BF),
            vm((pairs, 2 * nodes, LANES), BF),
            vm((pairs, LANES, 2 * nodes), BF),
            vm((slots, width), BF),
            vm((pairs, 2 * nodes, slots), F32),
            vm((pairs, 2 * nodes, slots), F32),
            vm((pairs, 2 * nodes, slots), BF),
            vm((pairs, 2 * nodes, slots), BF),
            vm((nodes, width), BF),
            dma((len(args),)),
            *([dma] * 15),
        ],
        compiler_params=pltpu.CompilerParams(
            collective_id=0, has_side_effects=True, vmem_limit_bytes=48 * 1024 * 1024
        ),
    )(*args)
    hidden, grad_pred, loss = pl.pallas_call(
        functools.partial(finish, slots // G),
        out_shape=(
            jax.ShapeDtypeStruct((1, nodes, width), BF),
            jax.ShapeDtypeStruct((variables, 1, points), F32),
            jax.ShapeDtypeStruct((1, 1), F32),
        ),
        in_specs=[vmem_spec] * 5,
        out_specs=(hbm_spec,) * 3,
        scratch_shapes=[vm((variables, 1, points), F32), vm((1, 1), F32), dma((4,))],
        compiler_params=pltpu.CompilerParams(vmem_limit_bytes=16 * 1024 * 1024),
    )(*parts)
    return hidden, jnp.transpose(grad_pred, (1, 0, 2)), loss.reshape(())


def solution(mesh):
    return jax.shard_map(
        functools.partial(local, mesh.shape["grid"], mesh.shape["member"]),
        mesh=mesh,
        in_specs=(
            P("member", None, "grid"),
            P(None, "grid"),
            P("grid"),
            P("grid", None),
            P("member", "grid", None),
            P("grid", None),
            P("grid"),
            P("grid", None),
            P("grid", None, None),
            P(),
            P(),
            P(),
            P(),
        ),
        out_specs=(P("member", "grid", None), P("member", None, "grid"), P()),
        check_vma=False,
    )
```

```python
import functools

import jax
import jax.numpy as jnp
from jax import lax
from jax.experimental import pallas as pl
from jax.experimental.pallas import tpu as pltpu
from jax.sharding import PartitionSpec as P

alpha_fair = 0.95
absent = -1e30
log2e = 1.4426950408889634
steep = 3e38

BF = jnp.bfloat16
F32 = jnp.float32
I32 = jnp.int32
LANES = 128
CHUNK = 32
GX, GZ = 4, 8


def dot(a, b, ca=1, cb=0):
    return lax.dot_general(a, b, (((ca,), (cb,)), ((), ())), preferred_element_type=F32)


def iota(shape, dim):
    return lax.broadcasted_iota(I32, shape, dim)


def lane_gather(x, idx):
    dims = lax.GatherDimensionNumbers(
        offset_dims=(),
        collapsed_slice_dims=(1,),
        start_index_map=(1,),
        operand_batching_dims=(0,),
        start_indices_batching_dims=(0,),
    )
    return lax.gather(
        x, idx[..., None], dims, (1, 1), mode=lax.GatherScatterMode.PROMISE_IN_BOUNDS
    )


def fair_coefficient(member_count):
    return alpha_fair / (2.0 * member_count * (member_count - 1)) + (1.0 - alpha_fair) / (
        2.0 * member_count * member_count
    )


def wait_bytes(ref, sem):
    pltpu.make_async_copy(ref, ref, sem).wait()


def kernel(
    grid_count,
    member_count,
    pred_h, truth_h, area_h, q_h, cot_h, es_h, ec_h, eb_h, sr_h, we_h, wq_h, wkv_h, wo_h,
    hid_o, base_o, recve, sel, area_o,
    predl, truth, area, q, cot, es_t, ec, eb, sr, we, wq, wkv, wo,
    pred, predp, wep, sendx, recvx, sende, crecv, csend, cret, lsend, lrecv,
    bias, qb, qst, ast, ww, qw, qw_t, aw, aw_t, values, s_scr, g_scr, gs_scr, wts, att,
    ld_sem, own_sem, fs, fr, cs, cr, rs, rr, ls, lr, bs, br, ws, wr, qs, qr,
):
    G, M = grid_count, member_count
    gi = lax.axis_index("grid")
    mi = lax.axis_index("member")
    variables, points = pred.shape
    nodes, width = q.shape
    pairs = width // LANES
    slots = sendx.shape[0]
    cap = slots // G
    fan = es_t.shape[0]
    coefficient = fair_coefficient(M)

    core = lax.rem(mi, 2)
    partner = mi + 1 - 2 * core
    wq_h = wq_h.at[:, pl.ds(pl.multiple_of(core * (width // 2), LANES), width // 2)]
    wkv_h = wkv_h.at[:, pl.ds(pl.multiple_of(core * width, LANES), width)]
    sources = [sr_h, pred_h, area_h, es_h, ec_h, eb_h, we_h, wkv_h, q_h, wq_h, cot_h, wo_h, truth_h]
    targets = [sr, predl, area, es_t, ec, eb, we, wkv, q, wq, cot, wo, truth]
    loads = [
        pltpu.make_async_copy(s, t, ld_sem.at[i]) for i, (s, t) in enumerate(zip(sources, targets))
    ]
    for c in loads[:6]:
        c.start()

    barrier = pltpu.get_barrier_semaphore()

    def turn(index, k, count):
        moved = index + k
        return jnp.where(moved >= count, moved - count, moved)

    gx, gz = lax.div(gi, GZ), lax.rem(gi, GZ)
    steps = [(dx, dz) for dx in range(GX) for dz in range(GZ)][1:]
    steps.sort(key=lambda d: -(min(d[0], GX - d[0]) + min(d[1], GZ - d[1])))
    tiles = [turn(gx, dx, GX) * GZ + turn(gz, dz, GZ) for dx, dz in steps]
    for peer in tiles:
        pl.semaphore_signal(barrier, inc=1, device_id={"grid": peer})
    for k in range(1, M):
        pl.semaphore_signal(barrier, inc=1, device_id={"member": turn(mi, k, M)})
    for c in loads[6:]:
        c.start()

    loads[0].wait()
    spots = jnp.broadcast_to(sr[0].astype(F32)[None], (G, cap, G)).reshape(slots, G)
    pick = iota((slots, G), 1) == (iota((slots, G), 0) // cap)
    rows = jnp.sum(jnp.where(pick, spots, 0.0), axis=1, keepdims=True).astype(I32)
    for c in range(slots // 64):
        r = pl.ds(64 * c, 64)
        hit = iota((64, points), 1) == rows[64 * c : 64 * c + 64]
        sel[r, :] = jnp.where(hit, 1.0, 0.0).astype(BF)
    predp[...] = jnp.zeros_like(predp)
    wep[...] = jnp.zeros_like(wep)
    for c in loads[1:6]:
        c.wait()
    pred[...] = predl[:, 0, :]
    predp[0:variables, :] = pred[...].astype(BF)
    tile_area = jnp.sum(area[...], axis=1, keepdims=True)
    lane = iota((slots, LANES), 1)
    sub = iota((slots, LANES), 0)
    x = dot(sel[...], predp[...], 1, 1)

    real = iota((fan, nodes), 0) < ec[...]
    es = jnp.where(real, es_t[...], -1).astype(F32).T.astype(I32)

    def spread_bias(start):
        r = slice(start, start + CHUNK)
        edges = es[r, :]
        slot_ids = iota((CHUNK, slots), 1)
        inverse = jnp.full((CHUNK, slots), -1, I32)
        for e in range(fan):
            inverse = jnp.where(edges[:, e : e + 1] == slot_ids, e, inverse)
        there = inverse >= 0
        index = jnp.maximum(inverse, 0)
        columns = [eb[r, j * LANES : (j + 1) * LANES] * log2e for j in range(4)]
        l = iota((CHUNK, LANES), 1)
        edge = l & (fan - 1)
        for t in range(4):
            place = (edge & 7) * 16 + 4 * t + (l >> 5)
            table = lane_gather(columns[0], place)
            for j in range(1, 4):
                table = jnp.where((edge >> 3) == j, lane_gather(columns[j], place), table)
            for hh in range(4):
                h = 4 * t + hh
                rows_of = slice((h % 2) * nodes + start, (h % 2) * nodes + start + CHUNK)
                for side in range(slots // LANES):
                    cols = slice(side * LANES, (side + 1) * LANES)
                    got = lane_gather(table, index[:, cols] + 32 * hh)
                    bias[h // 2, rows_of, cols] = jnp.where(
                        there[:, cols], got, absent
                    )

    for c in range(2):
        spread_bias(c * CHUNK)

    sendx[...] = jnp.where(lane == variables, tile_area, x)


    for c in loads[6:]:
        c.wait()
    pl.semaphore_wait(barrier, G - 1 + M - 1)
    for k in range(1, M):
        peer = turn(mi, k, M)
        pltpu.make_async_remote_copy(
            src_ref=pred.at[:, pl.ds(pl.multiple_of(peer * LANES, LANES), LANES)],
            dst_ref=crecv.at[mi],
            send_sem=cs,
            recv_sem=cr,
            device_id={"member": peer},
        ).start()
    own_lanes = pl.ds(pl.multiple_of(mi * LANES, LANES), LANES)
    own_chunk = pltpu.make_async_copy(pred.at[:, own_lanes], crecv.at[mi], own_sem)
    own_chunk.start()

    mine = pl.ds(pl.multiple_of(gi * cap, cap), cap)

    def send_grid(src, dst, s_sem, r_sem):
        for peer in tiles:
            theirs = pl.ds(pl.multiple_of(peer * cap, cap), cap)
            pltpu.make_async_remote_copy(
                src_ref=src.at[theirs],
                dst_ref=dst.at[mine],
                send_sem=s_sem,
                recv_sem=r_sem,
                device_id={"grid": peer},
            ).start()
        dst[mine, :] = src[mine, :]

    send_grid(sendx, recvx, fs, fr)

    def hand_over(ref, s_sem, r_sem):
        return pltpu.make_async_remote_copy(
            src_ref=ref.at[core],
            dst_ref=ref.at[core],
            send_sem=s_sem,
            recv_sem=r_sem,
            device_id={"member": partner},
        )

    wep[0:variables, :] = we[...]
    for c in range(width // 512):
        cols = slice(512 * c, 512 * c + 512)
        ww[core, :, cols] = dot(wep[...], wkv[:, cols]).astype(BF)
    hand_over(ww, ws, wr).start()
    qb[core] = (dot(q[...], wq[...]) * 0.125).astype(BF)

    hand_over(qb, qs, qr).start()


    half = LANES // 2
    for stacked in (qst, ast):
        stacked[...] = jnp.zeros_like(stacked)

    def stack_heads(p, block, stacked):
        stacked[p, 0:nodes, 0:half] = block[:, 0:half]
        stacked[p, nodes:, half:] = block[:, half:]

    for c in range(width // 512):
        cols = slice(512 * c, 512 * c + 512)
        grads = dot(cot[0], wo[cols, :], 1, 1).astype(BF)
        spread_bias((2 + c) * CHUNK)
        for k in range(4):
            stack_heads(4 * c + k, grads[:, k * LANES : (k + 1) * LANES], ast)
    wait_bytes(qb.at[0], qr)
    wait_bytes(ww.at[0], wr)
    for p in range(pairs):
        lanes = slice(p * LANES, (p + 1) * LANES)
        inner = slice((p % 4) * LANES, (p % 4 + 1) * LANES)
        stack_heads(p, qb[p // 4, :, inner], qst)
        for stacked, weights, by_node, by_field, factor in (
            (qst, ww[0, :, lanes], qw, qw_t, log2e),
            (ast, ww[1, :, lanes], aw, aw_t, 1.0),
        ):
            by_node[p] = (dot(stacked[p], weights, 1, 1) * factor).astype(BF)
            by_field[p] = dot(weights, stacked[p], 1, 1).astype(BF)

    wait_bytes(recvx.at[pl.ds(0, slots - cap)], fr)
    received = recvx[...]
    first = (lane == variables) & ((sub & (cap - 1)) == 0)
    total_area = jnp.sum(
        jnp.sum(jnp.where(first, received, 0.0), axis=0, keepdims=True), axis=1, keepdims=True
    )
    fields_t = received.T.astype(BF)

    def products(p):
        s_scr[p] = dot(qw[p], fields_t)
        g_scr[p] = dot(aw[p], fields_t)

    enc = jnp.zeros((LANES, slots), F32)
    def statistics():
        own_chunk.wait()
        wait_bytes(crecv.at[pl.ds(0, M - 1)], cr)

        own_area = area[:, own_lanes]
        part = jnp.zeros((1, LANES), F32)
        csend[:, variables // 16 * 16 :, :] = jnp.zeros((M, 16, LANES), BF)
        for row in range(0, variables, 16):
            r = slice(row, min(row + 16, variables))
            fields = [crecv[j, r, :] for j in range(M)]
            fact = truth[r, own_lanes]
            ranks = [jnp.zeros_like(fact) for _ in range(M)]
            skill = jnp.zeros_like(fact)
            for j in range(M):
                skill += jnp.abs(fields[j] - fact)
                for k in range(j + 1, M):
                    s = jnp.clip((fields[j] - fields[k]) * steep, -1.0, 1.0)
                    ranks[j] += s
                    ranks[k] -= s
            spread = sum(ranks[j] * fields[j] for j in range(M))
            crps = skill / M - (2.0 * coefficient) * spread
            part += jnp.sum(own_area * crps, axis=0, keepdims=True)
            for j in range(M):
                csend[j, r, :] = ranks[j].astype(BF)
        lsend[...] = jnp.broadcast_to(jnp.sum(part, axis=1, keepdims=True), lsend.shape)
        for k in range(1, M):
            pltpu.make_async_remote_copy(
                src_ref=lsend,
                dst_ref=lrecv.at[mi],
                send_sem=ls,
                recv_sem=lr,
                device_id={"member": turn(mi, k, M)},
            ).start()
        lrecv[mi] = lsend[...]
        for k in range(1, M):
            peer = turn(mi, k, M)
            pltpu.make_async_remote_copy(
                src_ref=csend.at[peer],
                dst_ref=cret.at[mi],
                send_sem=rs,
                recv_sem=rr,
                device_id={"member": peer},
            ).start()
        cret[mi] = csend[mi]

    products(0)
    for p in range(pairs):
        if p == 3:
            statistics()
        if p + 1 < pairs:
            products(p + 1)
        for i in range(2 * nodes // 64):
            r = slice(i * 64, (i + 1) * 64)
            s = s_scr[p, r, :] + bias[p, r, :]
            e = jnp.exp2(s - jnp.max(s, axis=1, keepdims=True))
            g = g_scr[p, r, :]
            share = 1.0 / jnp.sum(e, axis=1, keepdims=True)
            inner = jnp.sum(e * g, axis=1, keepdims=True) * share
            w = e * share
            wts[p, r, :] = w.astype(BF)
            gs_scr[p, r, :] = (w * (g - inner)).astype(BF)
        enc += dot(qw_t[p], gs_scr[p]) + dot(aw_t[p], wts[p])

    wait_bytes(lrecv.at[pl.ds(0, M - 1)], lr)
    tile_loss = jnp.sum(lrecv[:, 0, 0:1], axis=0, keepdims=True)
    sende[...] = jnp.where(lane == variables, tile_loss, enc.T)
    send_grid(sende, recve, bs, br)

    low = iota((nodes, LANES), 1) < half
    values[...] = dot(recvx[...].astype(BF), ww[1]).astype(BF)
    for p in range(pairs):
        both = dot(wts[p], values[:, p * LANES : (p + 1) * LANES])
        att[:, p * LANES : (p + 1) * LANES] = jnp.where(low, both[:nodes], both[nodes:]).astype(BF)
    hid_o[0] = (q[...].astype(F32) + dot(att[...], wo[...])).astype(BF)

    wait_bytes(cret.at[pl.ds(0, M - 1)], rr)
    area_o[...] = total_area
    scale = (points * G) / total_area
    for chunk in range(points // LANES):
        cols = slice(chunk * LANES, (chunk + 1) * LANES)
        d = pred[:, cols] - truth[:, cols]
        s = jnp.where(d > 0, 1.0, jnp.where(d < 0, -1.0, 0.0)) / M
        slope = s - (2.0 * coefficient) * cret[chunk, 0:variables, :].astype(F32)
        base_o[:, cols] = (area[:, cols] * scale) * slope

    wait_bytes(recve.at[pl.ds(0, slots - cap)], br)
    wait_bytes(sendx.at[pl.ds(0, slots - cap)], fs)
    wait_bytes(sende.at[pl.ds(0, slots - cap)], bs)
    wait_bytes(crecv.at[pl.ds(0, M - 1)], cs)
    wait_bytes(csend.at[pl.ds(0, M - 1)], rs)
    wait_bytes(lrecv.at[pl.ds(0, M - 1)], ls)
    wait_bytes(ww.at[0], ws)
    wait_bytes(qb.at[0], qs)


def finish(cap, hid, base, recve, sel, area, hid_o, grad_o, loss_o, grad, loss, sems):
    variables, points = base.shape
    copies = [pltpu.make_async_copy(hid, hid_o, sems.at[0])]
    copies[0].start()
    back = recve[...].T
    high = back.astype(BF)
    terms = jnp.concatenate([high, (back - high.astype(F32)).astype(BF)], axis=0)
    for c in range(points // 512):
        cols = slice(512 * c, 512 * c + 512)
        both = dot(terms, sel[:, cols])
        grad[:, 0, cols] = base[:, cols] + (both[:LANES] + both[LANES:])[:variables]
        copy = pltpu.make_async_copy(grad.at[:, :, cols], grad_o.at[:, :, cols], sems.at[2 + c])
        copy.start()
        copies.append(copy)
    back = recve[...]
    first = (iota(back.shape, 1) == variables) & ((iota(back.shape, 0) & (cap - 1)) == 0)
    total = jnp.sum(jnp.where(first, back, 0.0), axis=0, keepdims=True)
    loss[...] = jnp.sum(total, axis=1, keepdims=True) / (area[...] * variables)
    copy = pltpu.make_async_copy(loss, loss_o, sems.at[1])
    copy.start()
    for c in copies + [copy]:
        c.wait()


def local(
    grid_count, member_count,
    predictions, truth, area, queries, cotangent, edge_slot, edge_count, edge_bias, send_rows,
    w_embed, w_query, w_keyval, w_out,
):
    G, M = grid_count, member_count
    variables, points = truth.shape
    nodes, width = queries.shape
    slots = send_rows.shape[1] * send_rows.shape[2]
    pairs = width // LANES
    area = area.reshape(1, points)
    edge_count = edge_count.reshape(1, nodes)
    predictions = jnp.transpose(predictions, (1, 0, 2))
    edge_slot = edge_slot.T
    send_rows = jnp.transpose(send_rows, (0, 2, 1))
    args = (
        predictions, truth, area, queries, cotangent, edge_slot, edge_count, edge_bias, send_rows,
        w_embed, w_query, w_keyval, w_out,
    )
    args = tuple(pltpu.with_memory_space_constraint(a, pltpu.HBM) for a in args)
    rank_rows = (variables + 15) // 16 * 16
    hbm_spec = pl.BlockSpec(memory_space=pltpu.HBM)
    vmem_spec = pl.BlockSpec(memory_space=pltpu.VMEM)
    vm = pltpu.VMEM
    dma = pltpu.SemaphoreType.DMA
    shapes = [a.shape for a in args]
    shapes[10] = (width, width // 2)
    shapes[11] = (width, width)
    parts = pl.pallas_call(
        functools.partial(kernel, G, M),
        out_shape=(
            vm((1, nodes, width), BF),
            vm((variables, points), F32),
            vm((slots, LANES), F32),
            vm((slots, points), BF),
            vm((1, 1), F32),
        ),
        in_specs=[hbm_spec] * len(args),
        out_specs=(vmem_spec,) * 5,
        scratch_shapes=[vm(shape, a.dtype) for shape, a in zip(shapes, args)]
        + [
            vm((variables, points), F32),
            vm((LANES, points), BF),
            vm((LANES, width), BF),
            vm((slots, LANES), F32),
            vm((slots, LANES), F32),
            vm((slots, LANES), F32),
            vm((M, variables, LANES), F32),
            vm((M, rank_rows, LANES), BF),
            vm((M, rank_rows, LANES), BF),
            vm((8, LANES), F32),
            vm((M, 8, LANES), F32),
            vm((pairs, 2 * nodes, slots), F32),
            vm((2, nodes, width // 2), BF),
            vm((pairs, 2 * nodes, LANES), BF),
            vm((pairs, 2 * nodes, LANES), BF),
            vm((2, LANES, width), BF),
            vm((pairs, 2 * nodes, LANES), BF),
            vm((pairs, LANES, 2 * nodes), BF),
            vm((pairs, 2 * nodes, LANES), BF),
            vm((pairs, LANES, 2 * nodes), BF),
            vm((slots, width), BF),
            vm((pairs, 2 * nodes, slots), F32),
            vm((pairs, 2 * nodes, slots), F32),
            vm((pairs, 2 * nodes, slots), BF),
            vm((pairs, 2 * nodes, slots), BF),
            vm((nodes, width), BF),
            dma((len(args),)),
            *([dma] * 15),
        ],
        compiler_params=pltpu.CompilerParams(
            collective_id=0, has_side_effects=True, vmem_limit_bytes=48 * 1024 * 1024
        ),
    )(*args)
    hidden, grad_pred, loss = pl.pallas_call(
        functools.partial(finish, slots // G),
        out_shape=(
            jax.ShapeDtypeStruct((1, nodes, width), BF),
            jax.ShapeDtypeStruct((variables, 1, points), F32),
            jax.ShapeDtypeStruct((1, 1), F32),
        ),
        in_specs=[vmem_spec] * 5,
        out_specs=(hbm_spec,) * 3,
        scratch_shapes=[vm((variables, 1, points), F32), vm((1, 1), F32), dma((4,))],
        compiler_params=pltpu.CompilerParams(vmem_limit_bytes=16 * 1024 * 1024),
    )(*parts)
    return hidden, jnp.transpose(grad_pred, (1, 0, 2)), loss.reshape(())


def solution(mesh):
    return jax.shard_map(
        functools.partial(local, mesh.shape["grid"], mesh.shape["member"]),
        mesh=mesh,
        in_specs=(
            P("member", None, "grid"),
            P(None, "grid"),
            P("grid"),
            P("grid", None),
            P("member", "grid", None),
            P("grid", None),
            P("grid"),
            P("grid", None),
            P("grid", None, None),
            P(),
            P(),
            P(),
            P(),
        ),
        out_specs=(P("member", "grid", None), P("member", None, "grid"), P()),
        check_vma=False,
    )
```
